128 devices in a mesh: dp: 2 (over core), row: 8 (over x_lo, y), col: 8 (over z, x_hi).
Axes of the slice: x: 4 (x_hi: 2, x_lo: 2; x = x_hi * 2 + x_lo), y: 4, z: 4, core: 2. Of those that a mesh axis runs over, the one named last changes fastest.
Arguments:
- hidden: bfloat16 [2048, 28672], P(('dp', 'col'), 'row'), may hold values from -0.1875 to 0.1875
- cotangent: bfloat16 [2048, 8192], P(('dp', 'row'), 'col'), may hold values from -6 to 6
- language: int32 [2048], P(('dp', 'row')), may hold values from 0 to 31
- counts: int32 [32], replicated, may hold values from 128 to 2047
- weight: bfloat16 [28672, 8192], P('row', 'col'), may hold values from -0.0625 to 0.0625
Outputs:
- grad_hidden: bfloat16 [2048, 28672], P(('dp', 'col'), 'row')
- grad_weight: float32 [28672, 8192], P('row', ('col', 'dp'))
The draws below stay inside these ranges and needn't reach their ends.
All inputs are finite; a program needn't handle non-finite values.
Results may differ from the reference program's by a relative error of at most 0.013.
Values may be sent and summed in bfloat16 or wider, within the bound.
A program may use at most 256 MiB of HBM per device.

```python
import jax
import jax.numpy as jnp
from jax import lax

D = 8192
FF = 28672
LANGS = 32
TOKENS = 2048
N_DP = 2


def touch_ends(values, key, low, high):
    place = [jax.random.randint(jax.random.fold_in(key, axis), (), 0, length) for axis, length in enumerate(values.shape)]
    main_axis = values.shape.index(max(values.shape))
    next_to = place[:main_axis] + [(place[main_axis] + 1) % values.shape[main_axis]] + place[main_axis + 1:]
    return values.at[tuple(place)].set(low).at[tuple(next_to)].set(high)


def steps_of(own_key, shape, split, low, largest):
    loudness = 1.0
    for dim, blocks in split:
        steps = jax.random.uniform(jax.random.fold_in(jax.random.fold_in(own_key, 6), dim), (blocks,), jnp.float32, low / len(split), largest / len(split))
        loudness = loudness * jnp.repeat(jnp.exp(steps), shape[dim] // blocks).reshape((-1,) + (1,) * (len(shape) - 1 - dim))
    return loudness


def bell_draw(key, shape, spread, bound, pieces=(), held_as=jnp.bfloat16):
    factor_of = steps_of(key, shape, pieces, -0.22, 0.18) if pieces else 1.0
    drawn = jax.random.normal(key, shape, jnp.float32) * spread * factor_of
    return jnp.minimum(jnp.maximum(drawn, -bound), bound).astype(held_as)


def setup_inputs(seed: int = 0) -> dict:
    key_of = jax.random.split(jax.random.key(seed), 6)
    return {
        "hidden": bell_draw(key_of[0], (TOKENS, FF), 0.03, 0.1875, ((0, 16), (1, 8))),
        "cotangent": bell_draw(key_of[1], (TOKENS, D), 1.0, 6.0, ((0, 16), (1, 8))),
        "language": touch_ends(jax.random.randint(key_of[2], (TOKENS,), 0, LANGS), jax.random.fold_in(key_of[2], 1), 0, LANGS - 1).astype(jnp.int32),
        "counts": touch_ends(jax.random.randint(key_of[3], (LANGS,), 128, 2048), jax.random.fold_in(key_of[3], 1), 128, 2047).astype(jnp.int32),
        "weight": bell_draw(key_of[4], (FF, D), D ** -0.5, 0.0625, ((0, 8), (1, 8))),
    }


def reference(hidden, cotangent, language, counts, weight):
    lang_weight = jnp.sqrt(512.0 / counts.astype(jnp.float32))
    token_weight = lang_weight[language]
    scaled = (cotangent.astype(jnp.float32) * token_weight[:, None]).astype(jnp.bfloat16)
    grad_hidden = lax.dot_general(scaled, weight, (((1,), (1,)), ((), ())), preferred_element_type=jnp.float32).astype(jnp.bfloat16)
    replica_rows = TOKENS // N_DP
    grad_weight = jnp.zeros((FF, D), jnp.float32)
    for replica in range(N_DP):
        hidden_part = hidden[replica * replica_rows:(replica + 1) * replica_rows]
        scaled_part = scaled[replica * replica_rows:(replica + 1) * replica_rows]
        partial_value = lax.dot_general(hidden_part, scaled_part, (((0,), (0,)), ((), ())), preferred_element_type=jnp.float32)
        rounded = lax.optimization_barrier(partial_value.astype(jnp.bfloat16))
        grad_weight = grad_weight + rounded.astype(jnp.float32)
    return (grad_hidden, grad_weight)
```

```python
import jax
import jax.numpy as jnp
from jax import lax
from jax.experimental import pallas as pl
from jax.experimental.pallas import tpu as pltpu
from jax.sharding import PartitionSpec as P

MESH = pl.DeviceIdType.MESH
BF16 = jnp.bfloat16
F32 = jnp.float32

TOK = 128
FF = 3584
D = 1024
A = 2048
B = FF - A
AH = A // 2
BH = B // 2
TILE = 512
GT = 256
NG = FF // GT
MESSAGES = 64


def column(row_vector, n):
    on_diagonal = lax.broadcasted_iota(jnp.int32, (n, n), 0) == lax.broadcasted_iota(jnp.int32, (n, n), 1)
    return jnp.sum(jnp.where(on_diagonal, jnp.broadcast_to(row_vector, (n, n)), 0.0), axis=1, keepdims=True)


def kernel(
    h_ref, c_ref, lang_ref, counts_ref, w_ref,
    gh_ref, own_ref, other_ref,
    wv, ha, hb, call, pa, pb, ra2, ra1, rax, rbx, rb2, rb1, gst,
    ss, rs, gss, grs, gls, ls,
):
    dp, row, col = lax.axis_index("dp"), lax.axis_index("row"), lax.axis_index("col")
    xl, y = row // 4, row % 4
    z, h = col // 2, col % 2
    q = 1 - h
    zp, zm, zo = (z + 1) % 4, (z + 3) % 4, (z + 2) % 4
    yp, ym, yo = (y + 1) % 4, (y + 3) % 4, (y + 2) % 4
    to_zp, to_zm = (dp, row, zp * 2 + h), (dp, row, zm * 2 + h)
    to_x2 = (dp, row, z * 2 + q)
    to_yp, to_ym = (dp, xl * 4 + yp, col), (dp, xl * 4 + ym, col)
    to_xl = (dp, (1 - xl) * 4 + y, col)
    to_dp = (1 - dp, row, col)
    neighbours = (to_zp, to_zm, to_x2, to_yp, to_ym, to_xl, to_dp)

    barrier = pltpu.get_barrier_semaphore()
    for device in neighbours:
        pl.semaphore_signal(barrier, inc=1, device_id=device, device_id_type=MESH)

    load_w = pltpu.make_async_copy(w_ref, wv, ls.at[0])
    load_a = pltpu.make_async_copy(h_ref.at[:, pl.ds(0, A)], ha.at[col], ls.at[1])
    load_b = pltpu.make_async_copy(h_ref.at[:, pl.ds(A, B)], hb.at[col], ls.at[2])
    load_w.start()
    load_a.start()
    load_b.start()

    lang_weight = column(jnp.sqrt(512.0 / counts_ref[...].astype(F32)), 32)
    matches = lang_ref[...] == lax.broadcasted_iota(jnp.int32, (32, TOK), 0)
    weight_row = jnp.sum(jnp.where(matches, lang_weight, 0.0), axis=0, keepdims=True)
    token_weight = column(weight_row, TOK)
    call[row] = (c_ref[...].astype(F32) * token_weight).astype(BF16)

    pl.semaphore_wait(barrier, len(neighbours))

    sent = []

    def send(src, dst, device):
        i = len(sent)
        copy = pltpu.make_async_remote_copy(
            src_ref=src, dst_ref=dst, send_sem=ss.at[i], recv_sem=rs.at[i], device_id=device, device_id_type=MESH
        )
        copy.start()
        sent.append(copy)
        return copy

    def got(*copies):
        for copy in copies:
            copy.wait_recv()

    def pass_on(ref, block, device, lo=None, n=None):
        at = ref.at[block] if lo is None else ref.at[block, :, pl.ds(lo, n)]
        return send(at, at, device)

    h_a, h_b = h_ref.at[:, pl.ds(0, A)], h_ref.at[:, pl.ds(A, B)]
    own_b = [send(h_b, hb.at[col], d) for d in (to_zp, to_zm)]
    own_ax = send(h_a, ha.at[col], to_x2)
    own_cx = pass_on(call, row, to_xl)
    own_cy = [pass_on(call, row, d) for d in (to_yp, to_ym)]
    own_a = [send(h_a, ha.at[col], d) for d in (to_zp, to_zm)]

    def cblock(yy, partner):
        return ((1 - xl) if partner else xl) * 4 + yy

    def chalf(block, half, device):
        at = call.at[block, pl.ds(half * 64, 64), :]
        return send(at, at, device)

    got(own_cx)
    par_cy = [pass_on(call, cblock(y, True), d) for d in (to_yp, to_ym)]
    got(*own_cy)
    own_c2 = [chalf(cblock(ym, False), 0, to_yp), chalf(cblock(yp, False), 1, to_ym)]

    got(*own_b)
    fwd_b = [pass_on(hb, zm * 2 + h, to_zp, 0, BH), pass_on(hb, zp * 2 + h, to_zm, BH, BH)]
    x_b = [pass_on(hb, zm * 2 + h, to_x2), pass_on(hb, zp * 2 + h, to_x2), send(h_b, hb.at[col], to_x2)]

    got(own_ax)
    par_a = [pass_on(ha, z * 2 + q, d) for d in (to_zp, to_zm)]
    got(*par_cy)
    par_c2 = [chalf(cblock(ym, True), 0, to_yp), chalf(cblock(yp, True), 1, to_ym)]
    got(*own_a)
    fwd_a = [pass_on(ha, zm * 2 + h, to_zp, 0, AH), pass_on(ha, zp * 2 + h, to_zm, AH, AH)]
    got(*own_c2, *par_c2)
    load_w.wait()

    def partial_sums(at, zd):
        cots = call[pl.ds(zd * 2, 2)].reshape(2 * TOK, D)

        def tile(ref, base):
            def step(j, carry):
                rows = pl.ds(pl.multiple_of(base + j * TILE, TILE), TILE)
                part = lax.dot_general(cots, wv[rows, :], (((1,), (1,)), ((), ())), preferred_element_type=F32)
                part = part.astype(BF16).reshape(2, TOK, TILE)
                ref[at, :, :, pl.ds(pl.multiple_of(j * TILE, TILE), TILE)] = part
                return carry
            return step

        lax.fori_loop(0, A // TILE, tile(pa, 0), 0)
        lax.fori_loop(0, B // TILE, tile(pb, A), 0)

    partial_sums(0, zo)
    got(*fwd_b)
    x_b2 = [pass_on(hb, zo * 2 + h, to_x2, 0, BH), pass_on(hb, zo * 2 + h, to_x2, BH, BH)]
    partial_sums(1, zp)
    partial_sums(2, zm)
    got(*par_a)
    fwd_pa = [pass_on(ha, zm * 2 + q, to_zp, 0, AH), pass_on(ha, zp * 2 + q, to_zm, AH, AH)]
    partial_sums(3, z)

    def far_a(hh):
        return [
            send(pa.at[0, hh, :, pl.ds(0, AH)], ra2.at[hh, 0], to_zp),
            send(pa.at[0, hh, :, pl.ds(AH, AH)], ra2.at[hh, 1], to_zm),
        ]

    far_pa = far_a(q)
    cross_b = [send(pb.at[k, q], rbx.at[k], to_x2) for k in range(4)]
    far_oa = far_a(h)

    load_a.wait()
    load_b.wait()
    got(*fwd_a, *fwd_pa)

    def weight_tiles(ref, base, lo, hi):
        def step(j, carry):
            cols = pl.ds(pl.multiple_of(j * GT, GT), GT)
            hid = ref[:, :, cols].reshape(8 * TOK, GT)
            tile = base + j
            for half in range(2):
                cots = call[:, :, pl.ds(half * 512, 512)].reshape(8 * TOK, 512)
                out = lax.dot_general(hid, cots, (((0,), (0,)), ((), ())), preferred_element_type=F32)
                gst[tile, half] = out.astype(BF16)
            weight_copy(tile).start()
            weight_send(tile).start()
            return carry
        lax.fori_loop(lo, hi, step, 0)

    def weight_copy(tile):
        rows = pl.ds(pl.multiple_of(tile * GT, GT), GT)
        return pltpu.make_async_copy(gst.at[tile, dp], own_ref.at[rows, :], gls.at[tile])

    def weight_send(tile):
        rows = pl.ds(pl.multiple_of(tile * GT, GT), GT)
        return pltpu.make_async_remote_copy(
            src_ref=gst.at[tile, 1 - dp], dst_ref=other_ref.at[rows, :], send_sem=gss.at[tile],
            recv_sem=grs.at[tile], device_id=to_dp, device_id_type=MESH,
        )

    def add(ref, at, *others):
        total = ref[at].astype(F32)
        for other, other_at in others:
            total = total + other[other_at].astype(F32)
        ref[at] = total.astype(BF16)

    everything = slice(None)

    def near_a(hh):
        add(pa, (1, hh, everything, slice(0, AH)), (ra2, (hh, 0)))
        add(pa, (2, hh, everything, slice(AH, A)), (ra2, (hh, 1)))
        return [send(pa.at[1, hh], ra1.at[hh, 0], to_zp), send(pa.at[2, hh], ra1.at[hh, 1], to_zm)]

    weight_tiles(ha, 0, 0, 4)
    got(*far_pa)
    near_pa = near_a(q)
    got(cross_b[0])
    add(pb, (0, h), (rbx, 0))
    far_b = [
        send(pb.at[0, h, :, pl.ds(0, BH)], rb2.at[0], to_zp),
        send(pb.at[0, h, :, pl.ds(BH, BH)], rb2.at[1], to_zm),
    ]
    got(*far_oa)
    near_oa = near_a(h)
    weight_tiles(ha, 0, 4, A // GT)
    got(*x_b, *x_b2)
    weight_tiles(hb, A // GT, 0, 2)
    got(*near_pa)
    add(pa, (3, q), (ra1, (q, 0)), (ra1, (q, 1)))
    last_ax = send(pa.at[3, q], rax, to_x2)
    got(cross_b[1], cross_b[2], *far_b)
    add(pb, (1, h), (rbx, 1))
    add(pb, (1, h, everything, slice(0, BH)), (rb2, 0))
    add(pb, (2, h), (rbx, 2))
    add(pb, (2, h, everything, slice(BH, B)), (rb2, 1))
    near_b = [send(pb.at[1, h], rb1.at[0], to_zp), send(pb.at[2, h], rb1.at[1], to_zm)]
    weight_tiles(hb, A // GT, 2, B // GT)
    got(cross_b[3])
    add(pb, (3, h), (rbx, 3))
    got(*near_oa)
    add(pa, (3, h), (ra1, (h, 0)), (ra1, (h, 1)))
    got(last_ax)
    add(pa, (3, h), (rax, everything))
    out_a = pltpu.make_async_copy(pa.at[3, h], gh_ref.at[:, pl.ds(0, A)], ls.at[3])
    out_a.start()
    got(*near_b)
    add(pb, (3, h), (rb1, 0), (rb1, 1))
    out_b = pltpu.make_async_copy(pb.at[3, h], gh_ref.at[:, pl.ds(A, B)], ls.at[4])
    out_b.start()

    for copy in sent:
        copy.wait_send()

    def finish(tile, carry):
        weight_copy(tile).wait()
        weight_send(tile).wait()
        return carry

    lax.fori_loop(0, NG, finish, 0)
    out_a.wait()
    out_b.wait()


def body(hidden, cotangent, language, counts, weight):
    anywhere = pl.BlockSpec(memory_space=pl.ANY)
    vmem = pl.BlockSpec(memory_space=pltpu.VMEM)
    dma = pltpu.SemaphoreType.DMA
    grad_hidden, own, other = pl.pallas_call(
        kernel,
        out_shape=(
            jax.ShapeDtypeStruct((TOK, FF), BF16),
            jax.ShapeDtypeStruct((FF, D // 2), BF16),
            jax.ShapeDtypeStruct((FF, D // 2), BF16),
        ),
        in_specs=[anywhere, vmem, vmem, vmem, anywhere],
        out_specs=(anywhere, anywhere, anywhere),
        scratch_shapes=[
            pltpu.VMEM((FF, D), BF16),
            pltpu.VMEM((8, TOK, A), BF16),
            pltpu.VMEM((8, TOK, B), BF16),
            pltpu.VMEM((8, TOK, D), BF16),
            pltpu.VMEM((4, 2, TOK, A), BF16),
            pltpu.VMEM((4, 2, TOK, B), BF16),
            pltpu.VMEM((2, 2, TOK, AH), BF16),
            pltpu.VMEM((2, 2, TOK, A), BF16),
            pltpu.VMEM((TOK, A), BF16),
            pltpu.VMEM((4, TOK, B), BF16),
            pltpu.VMEM((2, TOK, BH), BF16),
            pltpu.VMEM((2, TOK, B), BF16),
            pltpu.VMEM((NG, 2, GT, D // 2), BF16),
            dma((MESSAGES,)),
            dma((MESSAGES,)),
            dma((NG,)),
            dma((NG,)),
            dma((NG,)),
            dma((5,)),
        ],
        compiler_params=pltpu.CompilerParams(
            collective_id=0, has_side_effects=True, vmem_limit_bytes=56 * 2**20
        ),
        cost_estimate=pl.CostEstimate(flops=4 * 1024 * FF * D, bytes_accessed=24 * 2**20, transcendentals=32),
    )(hidden, cotangent, language.reshape(1, TOK), counts.reshape(1, 32), weight)
    return grad_hidden, own.astype(F32) + other.astype(F32)


def solution(mesh):
    placed = (
        P(("dp", "col"), "row"),
        P(("dp", "row"), "col"),
        P(("dp", "row")),
        P(),
        P("row", "col"),
    )
    return jax.shard_map(
        body,
        mesh=mesh,
        in_specs=placed,
        out_specs=(P(("dp", "col"), "row"), P("row", ("col", "dp"))),
        check_vma=False,
    )
```

```python
import jax
import jax.numpy as jnp
from jax import lax
from jax.experimental import pallas as pl
from jax.experimental.pallas import tpu as pltpu
from jax.sharding import PartitionSpec as P

MESH = pl.DeviceIdType.MESH
BF16 = jnp.bfloat16
F32 = jnp.float32

TOK = 128
FF = 3584
D = 1024
A = 2048
B = FF - A
AH = A // 2
BH = B // 2
TILE = 512
GT = 256
NG = FF // GT
MESSAGES = 64


def column(row_vector, n):
    on_diagonal = lax.broadcasted_iota(jnp.int32, (n, n), 0) == lax.broadcasted_iota(jnp.int32, (n, n), 1)
    return jnp.sum(jnp.where(on_diagonal, jnp.broadcast_to(row_vector, (n, n)), 0.0), axis=1, keepdims=True)


def kernel(
    h_ref, c_ref, lang_ref, counts_ref, w_ref,
    gh_ref, gw_ref,
    wv, ha, hb, call, pa, pb, ra2, ra1, rax, rbx, rb2, rb1, gst, grv,
    ss, rs, gss, grs, ls,
):
    dp, row, col = lax.axis_index("dp"), lax.axis_index("row"), lax.axis_index("col")
    xl, y = row // 4, row % 4
    z, h = col // 2, col % 2
    q = 1 - h
    zp, zm, zo = (z + 1) % 4, (z + 3) % 4, (z + 2) % 4
    yp, ym, yo = (y + 1) % 4, (y + 3) % 4, (y + 2) % 4
    to_zp, to_zm = (dp, row, zp * 2 + h), (dp, row, zm * 2 + h)
    to_x2 = (dp, row, z * 2 + q)
    to_yp, to_ym = (dp, xl * 4 + yp, col), (dp, xl * 4 + ym, col)
    to_xl = (dp, (1 - xl) * 4 + y, col)
    to_dp = (1 - dp, row, col)
    neighbours = (to_zp, to_zm, to_x2, to_yp, to_ym, to_xl, to_dp)

    barrier = pltpu.get_barrier_semaphore()
    for device in neighbours:
        pl.semaphore_signal(barrier, inc=1, device_id=device, device_id_type=MESH)

    load_w = pltpu.make_async_copy(w_ref, wv, ls.at[0])
    load_a = pltpu.make_async_copy(h_ref.at[:, pl.ds(0, A)], ha.at[col], ls.at[1])
    load_b = pltpu.make_async_copy(h_ref.at[:, pl.ds(A, B)], hb.at[col], ls.at[2])
    load_w.start()
    load_a.start()
    load_b.start()

    lang_weight = column(jnp.sqrt(512.0 / counts_ref[...].astype(F32)), 32)
    matches = lang_ref[...] == lax.broadcasted_iota(jnp.int32, (32, TOK), 0)
    weight_row = jnp.sum(jnp.where(matches, lang_weight, 0.0), axis=0, keepdims=True)
    token_weight = column(weight_row, TOK)
    call[row] = (c_ref[...].astype(F32) * token_weight).astype(BF16)

    pl.semaphore_wait(barrier, len(neighbours))

    sent = []

    def send(src, dst, device):
        i = len(sent)
        copy = pltpu.make_async_remote_copy(
            src_ref=src, dst_ref=dst, send_sem=ss.at[i], recv_sem=rs.at[i], device_id=device, device_id_type=MESH
        )
        copy.start()
        sent.append(copy)
        return copy

    def got(*copies):
        for copy in copies:
            copy.wait_recv()

    def pass_on(ref, block, device, lo=None, n=None):
        at = ref.at[block] if lo is None else ref.at[block, :, pl.ds(lo, n)]
        return send(at, at, device)

    h_a, h_b = h_ref.at[:, pl.ds(0, A)], h_ref.at[:, pl.ds(A, B)]
    own_b = [send(h_b, hb.at[col], d) for d in (to_zp, to_zm)]
    own_ax = send(h_a, ha.at[col], to_x2)
    own_cx = pass_on(call, row, to_xl)
    own_cy = [pass_on(call, row, d) for d in (to_yp, to_ym)]
    own_a = [send(h_a, ha.at[col], d) for d in (to_zp, to_zm)]

    def cblock(yy, partner):
        return ((1 - xl) if partner else xl) * 4 + yy

    def chalf(block, half, device):
        at = call.at[block, pl.ds(half * 64, 64), :]
        return send(at, at, device)

    got(own_cx)
    par_cy = [pass_on(call, cblock(y, True), d) for d in (to_yp, to_ym)]
    got(*own_cy)
    own_c2 = [chalf(cblock(ym, False), 0, to_yp), chalf(cblock(yp, False), 1, to_ym)]

    got(*own_b)
    fwd_b = [pass_on(hb, zm * 2 + h, to_zp, 0, BH), pass_on(hb, zp * 2 + h, to_zm, BH, BH)]
    x_b = [pass_on(hb, zm * 2 + h, to_x2), pass_on(hb, zp * 2 + h, to_x2), send(h_b, hb.at[col], to_x2)]

    got(own_ax)
    par_a = [pass_on(ha, z * 2 + q, d) for d in (to_zp, to_zm)]
    got(*par_cy)
    par_c2 = [chalf(cblock(ym, True), 0, to_yp), chalf(cblock(yp, True), 1, to_ym)]
    got(*own_a)
    fwd_a = [pass_on(ha, zm * 2 + h, to_zp, 0, AH), pass_on(ha, zp * 2 + h, to_zm, AH, AH)]
    got(*own_c2, *par_c2)
    load_w.wait()

    def partial_sums(at, zd):
        cots = call[pl.ds(zd * 2, 2)].reshape(2 * TOK, D)

        def tile(ref, base):
            def step(j, carry):
                rows = pl.ds(pl.multiple_of(base + j * TILE, TILE), TILE)
                part = lax.dot_general(cots, wv[rows, :], (((1,), (1,)), ((), ())), preferred_element_type=F32)
                part = part.astype(BF16).reshape(2, TOK, TILE)
                ref[at, :, :, pl.ds(pl.multiple_of(j * TILE, TILE), TILE)] = part
                return carry
            return step

        lax.fori_loop(0, A // TILE, tile(pa, 0), 0)
        lax.fori_loop(0, B // TILE, tile(pb, A), 0)

    partial_sums(0, zo)
    got(*fwd_b)
    x_b2 = [pass_on(hb, zo * 2 + h, to_x2, 0, BH), pass_on(hb, zo * 2 + h, to_x2, BH, BH)]
    partial_sums(1, zp)
    partial_sums(2, zm)
    got(*par_a)
    fwd_pa = [pass_on(ha, zm * 2 + q, to_zp, 0, AH), pass_on(ha, zp * 2 + q, to_zm, AH, AH)]
    partial_sums(3, z)

    def far_a(hh):
        return [
            send(pa.at[0, hh, :, pl.ds(0, AH)], ra2.at[hh, 0], to_zp),
            send(pa.at[0, hh, :, pl.ds(AH, AH)], ra2.at[hh, 1], to_zm),
        ]

    far_pa = far_a(q)
    cross_b = [send(pb.at[k, q], rbx.at[k], to_x2) for k in range(4)]
    far_oa = far_a(h)

    load_a.wait()
    load_b.wait()
    got(*fwd_a, *fwd_pa)

    def weight_tiles(ref, base, lo, hi):
        def step(j, carry):
            cols = pl.ds(pl.multiple_of(j * GT, GT), GT)
            hid = ref[:, :, cols].reshape(8 * TOK, GT)
            tile = base + j

            def product(part):
                cots = call[:, :, pl.ds(pl.multiple_of(part * 512, 512), 512)].reshape(8 * TOK, 512)
                out = lax.dot_general(hid, cots, (((0,), (0,)), ((), ())), preferred_element_type=F32)
                return out.astype(BF16)

            gst[tile] = product(1 - dp)
            weight_send(tile).start()
            gw_ref[weight_rows(tile), :] = product(dp).astype(F32)
            return carry
        lax.fori_loop(lo, hi, step, 0)

    def weight_rows(tile):
        return pl.ds(pl.multiple_of(tile * GT, GT), GT)

    def weight_send(tile):
        return pltpu.make_async_remote_copy(
            src_ref=gst.at[tile], dst_ref=grv.at[tile], send_sem=gss.at[tile],
            recv_sem=grs.at[tile], device_id=to_dp, device_id_type=MESH,
        )

    def weight_sum(tile, carry):
        weight_send(tile).wait()
        gw_ref[weight_rows(tile), :] += grv[tile].astype(F32)
        return carry

    def add(ref, at, *others):
        total = ref[at].astype(F32)
        for other, other_at in others:
            total = total + other[other_at].astype(F32)
        ref[at] = total.astype(BF16)

    everything = slice(None)

    def near_a(hh):
        add(pa, (1, hh, everything, slice(0, AH)), (ra2, (hh, 0)))
        add(pa, (2, hh, everything, slice(AH, A)), (ra2, (hh, 1)))
        return [send(pa.at[1, hh], ra1.at[hh, 0], to_zp), send(pa.at[2, hh], ra1.at[hh, 1], to_zm)]

    weight_tiles(ha, 0, 0, 4)
    got(*far_pa)
    near_pa = near_a(q)
    got(cross_b[0])
    add(pb, (0, h), (rbx, 0))
    far_b = [
        send(pb.at[0, h, :, pl.ds(0, BH)], rb2.at[0], to_zp),
        send(pb.at[0, h, :, pl.ds(BH, BH)], rb2.at[1], to_zm),
    ]
    got(*far_oa)
    near_oa = near_a(h)
    weight_tiles(ha, 0, 4, A // GT)
    got(*x_b, *x_b2)
    weight_tiles(hb, A // GT, 0, 2)
    got(*near_pa)
    add(pa, (3, q), (ra1, (q, 0)), (ra1, (q, 1)))
    last_ax = send(pa.at[3, q], rax, to_x2)
    got(cross_b[1], cross_b[2], *far_b)
    add(pb, (1, h), (rbx, 1))
    add(pb, (1, h, everything, slice(0, BH)), (rb2, 0))
    add(pb, (2, h), (rbx, 2))
    add(pb, (2, h, everything, slice(BH, B)), (rb2, 1))
    near_b = [send(pb.at[1, h], rb1.at[0], to_zp), send(pb.at[2, h], rb1.at[1], to_zm)]
    weight_tiles(hb, A // GT, 2, B // GT)
    lax.fori_loop(0, NG, weight_sum, 0)
    got(cross_b[3])
    add(pb, (3, h), (rbx, 3))
    got(*near_oa)
    add(pa, (3, h), (ra1, (h, 0)), (ra1, (h, 1)))
    got(last_ax)
    add(pa, (3, h), (rax, everything))
    gh_ref[:, 0:A] = pa[3, h]
    got(*near_b)
    add(pb, (3, h), (rb1, 0), (rb1, 1))
    gh_ref[:, A:FF] = pb[3, h]

    for copy in sent:
        copy.wait_send()


def body(hidden, cotangent, language, counts, weight):
    anywhere = pl.BlockSpec(memory_space=pl.ANY)
    vmem = pl.BlockSpec(memory_space=pltpu.VMEM)
    dma = pltpu.SemaphoreType.DMA
    return pl.pallas_call(
        kernel,
        out_shape=(pltpu.VMEM((TOK, FF), BF16), pltpu.VMEM((FF, D // 2), F32)),
        in_specs=[anywhere, vmem, vmem, vmem, anywhere],
        out_specs=(vmem, vmem),
        scratch_shapes=[
            pltpu.VMEM((FF, D), BF16),
            pltpu.VMEM((8, TOK, A), BF16),
            pltpu.VMEM((8, TOK, B), BF16),
            pltpu.VMEM((8, TOK, D), BF16),
            pltpu.VMEM((4, 2, TOK, A), BF16),
            pltpu.VMEM((4, 2, TOK, B), BF16),
            pltpu.VMEM((2, 2, TOK, AH), BF16),
            pltpu.VMEM((2, 2, TOK, A), BF16),
            pltpu.VMEM((TOK, A), BF16),
            pltpu.VMEM((4, TOK, B), BF16),
            pltpu.VMEM((2, TOK, BH), BF16),
            pltpu.VMEM((2, TOK, B), BF16),
            pltpu.VMEM((NG, GT, D // 2), BF16),
            pltpu.VMEM((NG, GT, D // 2), BF16),
            dma((MESSAGES,)),
            dma((MESSAGES,)),
            dma((NG,)),
            dma((NG,)),
            dma((3,)),
        ],
        compiler_params=pltpu.CompilerParams(
            collective_id=0, has_side_effects=True, vmem_limit_bytes=54 * 2**20
        ),
        cost_estimate=pl.CostEstimate(flops=4 * 1024 * FF * D, bytes_accessed=24 * 2**20, transcendentals=32),
    )(hidden, cotangent, language.reshape(1, TOK), counts.reshape(1, 32), weight)


def solution(mesh):
    placed = (
        P(("dp", "col"), "row"),
        P(("dp", "row"), "col"),
        P(("dp", "row")),
        P(),
        P("row", "col"),
    )
    return jax.shard_map(
        body,
        mesh=mesh,
        in_specs=placed,
        out_specs=(P(("dp", "col"), "row"), P("row", ("col", "dp"))),
        check_vma=False,
    )
```

```python
import jax
import jax.numpy as jnp
from jax import lax
from jax.experimental import pallas as pl
from jax.experimental.pallas import tpu as pltpu
from jax.sharding import PartitionSpec as P

MESH = pl.DeviceIdType.MESH
BF16 = jnp.bfloat16
F32 = jnp.float32

TOK = 128
FF = 3584
D = 1024
DH = D // 2
A = 1536
S = 1024
FT = 512
GT = 256
NA, NS = A // GT, S // GT
NW = 2
WR = S // 2 // NW
MESSAGES = 80


def column(row_vector, n):
    on_diagonal = lax.broadcasted_iota(jnp.int32, (n, n), 0) == lax.broadcasted_iota(jnp.int32, (n, n), 1)
    return jnp.sum(jnp.where(on_diagonal, jnp.broadcast_to(row_vector, (n, n)), 0.0), axis=1, keepdims=True)


def kernel(
    h_ref, c_ref, lang_ref, counts_ref, w_ref,
    gh_ref, gw_ref,
    wa, ws, wx, ha, hs, call, pa, ps, ra2, rs2, ra1, rs1, rax, rsx, gst, grv, xst, xrv, xsum, xin,
    ss, rs, gss, grs, xss, xrs, ls,
):
    dp, row, col = lax.axis_index("dp"), lax.axis_index("row"), lax.axis_index("col")
    xl, y = row // 4, row % 4
    z, h = col // 2, col % 2
    q = 1 - h
    x = h * 2 + xl
    xp, xm, xo = (x + 1) % 4, (x + 3) % 4, (x + 2) % 4
    zp, zm, zo = (z + 1) % 4, (z + 3) % 4, (z + 2) % 4
    yp, ym, yo = (y + 1) % 4, (y + 3) % 4, (y + 2) % 4

    def device(at_x, at_y, at_z):
        return (dp, (at_x % 2) * 4 + at_y, at_z * 2 + at_x // 2)

    to_zp, to_zm = device(x, y, zp), device(x, y, zm)
    to_yp, to_ym = device(x, yp, z), device(x, ym, z)
    to_xp, to_xm, to_x2 = device(xp, y, z), device(xm, y, z), device(xo, y, z)
    to_dp = (1 - dp, row, col)
    neighbours = (to_zp, to_zm, to_yp, to_ym, to_xp, to_xm, to_x2, to_dp)

    barrier = pltpu.get_barrier_semaphore()
    for neighbour in neighbours:
        pl.semaphore_signal(barrier, inc=1, device_id=neighbour, device_id_type=MESH)

    s_own = pl.multiple_of(A + S * h, S // 2)
    s_other = pl.multiple_of(A + S * q, S // 2)
    h_a, h_s, h_o = (h_ref.at[:, pl.ds(at, n)] for at, n in ((0, A), (s_own, S), (s_other, S)))
    loads = [
        pltpu.make_async_copy(h_a, ha.at[col], ls.at[0]),
        pltpu.make_async_copy(h_s, hs.at[col], ls.at[1]),
        pltpu.make_async_copy(w_ref.at[pl.ds(0, A), :], wa, ls.at[2]),
        pltpu.make_async_copy(w_ref.at[pl.ds(s_own, S), :], ws, ls.at[3]),
    ]
    for load in loads:
        load.start()

    lang_weight = column(jnp.sqrt(512.0 / counts_ref[...].astype(F32)), 32)
    matches = lang_ref[...] == lax.broadcasted_iota(jnp.int32, (32, TOK), 0)
    weight_row = jnp.sum(jnp.where(matches, lang_weight, 0.0), axis=0, keepdims=True)
    token_weight = column(weight_row, TOK)
    call[h, row] = (c_ref[...].astype(F32) * token_weight).astype(BF16)

    pl.semaphore_wait(barrier, len(neighbours))

    sent = []

    def send(src, dst, to):
        i = len(sent)
        copy = pltpu.make_async_remote_copy(
            src_ref=src, dst_ref=dst, send_sem=ss.at[i], recv_sem=rs.at[i], device_id=to, device_id_type=MESH
        )
        copy.start()
        sent.append(copy)
        return copy

    def got(*copies):
        for copy in copies:
            copy.wait_recv()

    def cots_whole(at_x, at_y, to):
        at = call.at[at_x // 2, (at_x % 2) * 4 + at_y]
        return send(at, at, to)

    def cots_half(at_x, at_y, half, to):
        at = call.at[at_x // 2, (at_x % 2) * 4 + at_y, pl.ds(half * (TOK // 2), TOK // 2), :]
        return send(at, at, to)

    def cots_along_y(at_x):
        return [cots_whole(at_x, y, to_yp), cots_whole(at_x, y, to_ym)]

    def cots_far_y(at_x):
        return [cots_half(at_x, ym, 0, to_yp), cots_half(at_x, yp, 1, to_ym)]

    def hidden_on(ref, hh, n):
        half = n // 2
        at_m, at_p = (ref.at[zz * 2 + hh, :, pl.ds(lo, half)] for zz, lo in ((zm, 0), (zp, half)))
        return [send(at_m, at_m, to_zp), send(at_p, at_p, to_zm)]

    def hidden_round(src, ref, at):
        return [send(src, ref.at[at], to_zp), send(src, ref.at[at], to_zm)]

    par = z * 2 + q
    c_x = [cots_whole(x, y, to_xp), cots_whole(x, y, to_xm)]
    own_a = hidden_round(h_a, ha, col)
    x_a = send(h_a, ha.at[col], to_x2)
    c_y = cots_along_y(x)
    own_s = hidden_round(h_s, hs, col)
    x_s = send(h_o, hs.at[col], to_x2)

    got(*c_x)
    c_x2 = [cots_half(xm, y, 0, to_xp), cots_half(xp, y, 1, to_xm)]
    c_ym, c_yp = cots_along_y(xm), cots_along_y(xp)
    got(*c_y)
    c_y2 = cots_far_y(x)
    got(*own_a)
    far_own_a = hidden_on(ha, h, A)
    got(x_a)
    par_a = hidden_round(ha.at[par], ha, par)
    got(*c_x2)
    c_yo = cots_along_y(xo)
    got(*own_s)
    far_own_s = hidden_on(hs, h, S)
    got(x_s)
    par_s = hidden_round(hs.at[par], hs, par)
    w_x = []
    for i in range(NW):
        rows = pl.multiple_of(dp * (S // 2) + i * WR, WR)
        w_x.append(send(w_ref.at[pl.ds(pl.multiple_of(s_other + rows, WR), WR), :], wx.at[pl.ds(rows, WR), :], to_x2))
    got(*c_ym)
    c_ym2 = cots_far_y(xm)
    got(*c_yp)
    c_yp2 = cots_far_y(xp)
    got(*par_a)
    far_par_a = hidden_on(ha, q, A)
    got(*c_yo)
    c_yo2 = cots_far_y(xo)
    for load in loads:
        load.wait()
    got(*par_s)
    far_par_s = hidden_on(hs, q, S)
    got(*c_y2, *c_ym2, *c_yp2, *c_yo2)

    def times_weight(cots, weight):
        return lax.dot_general(cots, weight, (((1,), (1,)), ((), ())), preferred_element_type=F32)

    def cots_of(hh, zd):
        return call[hh, pl.ds(zd * 2, 2)].reshape(2 * TOK, D)

    def terms_a(at, zd):
        def step(j, carry):
            units = pl.ds(pl.multiple_of(j * FT, FT), FT)
            pa[at, :, :, units] = times_weight(cots_of(h, zd), wa[units, :]).astype(BF16).reshape(2, TOK, FT)
            return carry
        lax.fori_loop(0, A // FT, step, 0)

    def terms_s(at, zd):
        def step(j, carry):
            units = pl.ds(pl.multiple_of(j * FT, FT), FT)
            both = times_weight(cots_of(h, zd), ws[units, :]) + times_weight(cots_of(q, zd), wx[units, :])
            ps[at, :, :, units] = both.astype(BF16).reshape(2, TOK, FT)
            return carry
        lax.fori_loop(0, S // FT, step, 0)

    def add(ref, at, *others):
        total = ref[at].astype(F32)
        for other, other_at in others:
            total = total + other[other_at].astype(F32)
        ref[at] = total.astype(BF16)

    everything = slice(None)

    def far(p, r2, hh, n):
        half = n // 2
        return [
            send(p.at[0, hh, :, pl.ds(0, half)], r2.at[hh, 0], to_zp),
            send(p.at[0, hh, :, pl.ds(half, half)], r2.at[hh, 1], to_zm),
        ]

    def near(p, r2, r1, hh, n):
        half = n // 2
        add(p, (1, hh, everything, slice(0, half)), (r2, (hh, 0)))
        add(p, (2, hh, everything, slice(half, n)), (r2, (hh, 1)))
        return [send(p.at[1, hh], r1.at[hh, 0], to_zp), send(p.at[2, hh], r1.at[hh, 1], to_zm)]

    def home(p, r1, hh):
        add(p, (3, hh), (r1, (hh, 0)), (r1, (hh, 1)))

    terms_a(0, zo)
    far_aq = far(pa, ra2, q, A)
    far_ah = far(pa, ra2, h, A)
    terms_a(1, zp)
    terms_a(2, zm)
    w_dp = []
    for i in range(NW):
        got(w_x[i])
        rows = pl.ds(pl.multiple_of(dp * (S // 2) + i * WR, WR), WR)
        w_dp.append(send(wx.at[rows, :], wx.at[rows, :], to_dp))
    got(*w_dp)
    terms_s(0, zo)
    far_sq = far(ps, rs2, q, S)
    far_sh = far(ps, rs2, h, S)
    got(*far_aq)
    near_aq = near(pa, ra2, ra1, q, A)
    terms_s(1, zp)
    terms_s(2, zm)

    def product(ref, j, hh, part):
        hidden = ref[:, :, pl.ds(pl.multiple_of(j * GT, GT), GT)].reshape(8 * TOK, GT)
        cots = call[hh, :, :, pl.ds(pl.multiple_of(part * DH, DH), DH)].reshape(8 * TOK, DH)
        out = lax.dot_general(hidden, cots, (((0,), (0,)), ((), ())), preferred_element_type=F32)
        return out.astype(BF16)

    def to_other_core(st, rv, s_sem, r_sem, j):
        return pltpu.make_async_remote_copy(
            src_ref=st.at[j], dst_ref=rv.at[j], send_sem=s_sem.at[j], recv_sem=r_sem.at[j],
            device_id=to_dp, device_id_type=MESH,
        )

    def partner_tile(j, carry):
        xst[j] = product(hs, j, q, 1 - dp)
        to_other_core(xst, xrv, xss, xrs, j).start()
        xsum[j] = product(hs, j, q, dp)
        return carry

    def own_tiles(ref, base, first, n):
        def step(j, carry):
            gst[base + j] = product(ref, j, h, 1 - dp)
            to_other_core(gst, grv, gss, grs, base + j).start()
            gw_ref[pl.ds(pl.multiple_of(first + j * GT, GT), GT), :] = product(ref, j, h, dp).astype(F32)
            return carry
        lax.fori_loop(0, n, step, 0)

    def own_sums(base, first, n):
        def step(j, carry):
            to_other_core(gst, grv, gss, grs, base + j).wait()
            gw_ref[pl.ds(pl.multiple_of(first + j * GT, GT), GT), :] += grv[base + j].astype(F32)
            return carry
        lax.fori_loop(0, n, step, 0)

    got(*far_own_s, *far_par_s)
    lax.fori_loop(0, NS, partner_tile, 0)
    got(*far_sq)
    near_sq = near(ps, rs2, rs1, q, S)
    got(*far_ah)
    near_ah = near(pa, ra2, ra1, h, A)
    returns = []
    for j in range(NS):
        to_other_core(xst, xrv, xss, xrs, j).wait()
        add(xsum, j, (xrv, j))
        returns.append(send(xsum.at[j], xin.at[j], to_x2))
    got(*far_sh)
    near_sh = near(ps, rs2, rs1, h, S)
    terms_a(3, z)
    terms_s(3, z)
    got(*far_own_a, *far_par_a)
    own_tiles(hs, NA, s_own, NS)
    got(*near_aq)
    home(pa, ra1, q)
    last_a = send(pa.at[3, q], rax, to_x2)
    own_tiles(ha, 0, 0, NA)
    got(*near_sq)
    home(ps, rs1, q)
    last_s = send(ps.at[3, q], rsx, to_x2)
    own_sums(0, 0, NA)
    own_sums(NA, s_own, NS)
    got(*near_ah)
    home(pa, ra1, h)
    for j in range(NS):
        got(returns[j])
        gw_ref[pl.ds(pl.multiple_of(s_other + j * GT, GT), GT), :] = xin[j].astype(F32)
    got(*near_sh)
    home(ps, rs1, h)
    gh_ref[:, pl.ds(s_own, S)] = ps[3, h]
    got(last_a)
    add(pa, (3, h), (rax, everything))
    gh_ref[:, 0:A] = pa[3, h]
    got(last_s)
    gh_ref[:, pl.ds(s_other, S)] = rsx[...]

    for copy in sent:
        copy.wait_send()


def body(hidden, cotangent, language, counts, weight):
    anywhere = pl.BlockSpec(memory_space=pl.ANY)
    vmem = pl.BlockSpec(memory_space=pltpu.VMEM)
    dma = pltpu.SemaphoreType.DMA
    return pl.pallas_call(
        kernel,
        out_shape=(pltpu.VMEM((TOK, FF), BF16), pltpu.VMEM((FF, DH), F32)),
        in_specs=[anywhere, vmem, vmem, vmem, anywhere],
        out_specs=(vmem, vmem),
        scratch_shapes=[
            pltpu.VMEM((A, D), BF16),
            pltpu.VMEM((S, D), BF16),
            pltpu.VMEM((S, D), BF16),
            pltpu.VMEM((8, TOK, A), BF16),
            pltpu.VMEM((8, TOK, S), BF16),
            pltpu.VMEM((2, 8, TOK, D), BF16),
            pltpu.VMEM((4, 2, TOK, A), BF16),
            pltpu.VMEM((4, 2, TOK, S), BF16),
            pltpu.VMEM((2, 2, TOK, A // 2), BF16),
            pltpu.VMEM((2, 2, TOK, S // 2), BF16),
            pltpu.VMEM((2, 2, TOK, A), BF16),
            pltpu.VMEM((2, 2, TOK, S), BF16),
            pltpu.VMEM((TOK, A), BF16),
            pltpu.VMEM((TOK, S), BF16),
            pltpu.VMEM((NA + NS, GT, DH), BF16),
            pltpu.VMEM((NA + NS, GT, DH), BF16),
            pltpu.VMEM((NS, GT, DH), BF16),
            pltpu.VMEM((NS, GT, DH), BF16),
            pltpu.VMEM((NS, GT, DH), BF16),
            pltpu.VMEM((NS, GT, DH), BF16),
            dma((MESSAGES,)),
            dma((MESSAGES,)),
            dma((NA + NS,)),
            dma((NA + NS,)),
            dma((NS,)),
            dma((NS,)),
            dma((4,)),
        ],
        compiler_params=pltpu.CompilerParams(
            collective_id=0, has_side_effects=True, vmem_limit_bytes=54 * 2**20
        ),
        cost_estimate=pl.CostEstimate(flops=4 * 1024 * FF * D, bytes_accessed=24 * 2**20, transcendentals=32),
    )(hidden, cotangent, language.reshape(1, TOK), counts.reshape(1, 32), weight)


def solution(mesh):
    placed = (
        P(("dp", "col"), "row"),
        P(("dp", "row"), "col"),
        P(("dp", "row")),
        P(),
        P("row", "col"),
    )
    return jax.shard_map(
        body,
        mesh=mesh,
        in_specs=placed,
        out_specs=(P(("dp", "col"), "row"), P("row", ("col", "dp"))),
        check_vma=False,
    )
```

```python
import jax
import jax.numpy as jnp
from jax import lax
from jax.experimental import pallas as pl
from jax.experimental.pallas import tpu as pltpu
from jax.sharding import PartitionSpec as P

MESH = pl.DeviceIdType.MESH
BF16 = jnp.bfloat16
F32 = jnp.float32

TOK = 128
FF = 3584
D = 1024
DH = D // 2
A = 1536
S = 1024
FT = 512
GT = 256
NA, NS = A // GT, S // GT
NW = 2
WR = S // 2 // NW
MESSAGES = 80


def column(row_vector, n):
    on_diagonal = lax.broadcasted_iota(jnp.int32, (n, n), 0) == lax.broadcasted_iota(jnp.int32, (n, n), 1)
    return jnp.sum(jnp.where(on_diagonal, jnp.broadcast_to(row_vector, (n, n)), 0.0), axis=1, keepdims=True)


def kernel(
    h_ref, c_ref, lang_ref, counts_ref, w_ref,
    gh_ref, gw_ref,
    wa, ws, wx, ha, hs, call, pa, ps, ra2, rs2, ra1, rs1, rax, rsx, gst, grv, xst, xrv, xsum, xin,
    ss, rs, gss, grs, xss, xrs, ls,
):
    dp, row, col = lax.axis_index("dp"), lax.axis_index("row"), lax.axis_index("col")
    xl, y = row // 4, row % 4
    z, h = col // 2, col % 2
    q = 1 - h
    x = h * 2 + xl
    xp, xm, xo = (x + 1) % 4, (x + 3) % 4, (x + 2) % 4
    zp, zm, zo = (z + 1) % 4, (z + 3) % 4, (z + 2) % 4
    yp, ym, yo = (y + 1) % 4, (y + 3) % 4, (y + 2) % 4

    def device(at_x, at_y, at_z):
        return (dp, (at_x % 2) * 4 + at_y, at_z * 2 + at_x // 2)

    to_zp, to_zm = device(x, y, zp), device(x, y, zm)
    to_yp, to_ym = device(x, yp, z), device(x, ym, z)
    to_xp, to_xm, to_x2 = device(xp, y, z), device(xm, y, z), device(xo, y, z)
    to_dp = (1 - dp, row, col)
    neighbours = (to_zp, to_zm, to_yp, to_ym, to_xp, to_xm, to_x2, to_dp)

    barrier = pltpu.get_barrier_semaphore()
    for neighbour in neighbours:
        pl.semaphore_signal(barrier, inc=1, device_id=neighbour, device_id_type=MESH)

    s_own = pl.multiple_of(A + S * h, S // 2)
    s_other = pl.multiple_of(A + S * q, S // 2)
    h_a, h_s, h_o = (h_ref.at[:, pl.ds(at, n)] for at, n in ((0, A), (s_own, S), (s_other, S)))
    loads = [
        pltpu.make_async_copy(h_a, ha.at[col], ls.at[0]),
        pltpu.make_async_copy(h_s, hs.at[col], ls.at[1]),
        pltpu.make_async_copy(w_ref.at[pl.ds(0, A), :], wa, ls.at[2]),
        pltpu.make_async_copy(w_ref.at[pl.ds(s_own, S), :], ws, ls.at[3]),
    ]
    for load in loads:
        load.start()

    lang_weight = column(jnp.sqrt(512.0 / counts_ref[...].astype(F32)), 32)
    matches = lang_ref[...] == lax.broadcasted_iota(jnp.int32, (32, TOK), 0)
    weight_row = jnp.sum(jnp.where(matches, lang_weight, 0.0), axis=0, keepdims=True)
    token_weight = column(weight_row, TOK)
    call[h, row] = (c_ref[...].astype(F32) * token_weight).astype(BF16)

    pl.semaphore_wait(barrier, len(neighbours))

    sent = []

    def send(src, dst, to):
        i = len(sent)
        copy = pltpu.make_async_remote_copy(
            src_ref=src, dst_ref=dst, send_sem=ss.at[i], recv_sem=rs.at[i], device_id=to, device_id_type=MESH
        )
        copy.start()
        sent.append(copy)
        return copy

    def got(*copies):
        for copy in copies:
            copy.wait_recv()

    def cots_whole(at_x, at_y, to):
        at = call.at[at_x // 2, (at_x % 2) * 4 + at_y]
        return send(at, at, to)

    def cots_half(at_x, at_y, half, to):
        at = call.at[at_x // 2, (at_x % 2) * 4 + at_y, pl.ds(half * (TOK // 2), TOK // 2), :]
        return send(at, at, to)

    def cots_along_y(at_x):
        return [cots_whole(at_x, y, to_yp), cots_whole(at_x, y, to_ym)]

    def cots_far_y(at_x):
        return [cots_half(at_x, ym, 0, to_yp), cots_half(at_x, yp, 1, to_ym)]

    def hidden_on(ref, hh, n):
        half = n // 2
        at_m, at_p = (ref.at[zz * 2 + hh, :, pl.ds(lo, half)] for zz, lo in ((zm, 0), (zp, half)))
        return [send(at_m, at_m, to_zp), send(at_p, at_p, to_zm)]

    def hidden_round(src, ref, at):
        return [send(src, ref.at[at], to_zp), send(src, ref.at[at], to_zm)]

    par = z * 2 + q
    c_x = [cots_whole(x, y, to_xp), cots_whole(x, y, to_xm)]
    own_s = hidden_round(h_s, hs, col)
    c_y = cots_along_y(x)
    x_s = send(h_o, hs.at[col], to_x2)
    own_a = hidden_round(h_a, ha, col)

    got(*c_x)
    c_x2 = [cots_half(xm, y, 0, to_xp), cots_half(xp, y, 1, to_xm)]
    c_ym, c_yp = cots_along_y(xm), cots_along_y(xp)
    x_a = send(h_a, ha.at[col], to_x2)
    w_x = []
    for i in range(NW):
        rows = pl.multiple_of(dp * (S // 2) + i * WR, WR)
        w_x.append(send(w_ref.at[pl.ds(pl.multiple_of(s_other + rows, WR), WR), :], wx.at[pl.ds(rows, WR), :], to_x2))
    got(*own_s)
    far_own_s = hidden_on(hs, h, S)
    got(*c_y)
    c_y2 = cots_far_y(x)
    got(x_s)
    par_s = hidden_round(hs.at[par], hs, par)
    got(*c_x2)
    c_yo = cots_along_y(xo)
    got(*own_a)
    got(*c_ym)
    c_ym2 = cots_far_y(xm)
    got(*c_yp)
    c_yp2 = cots_far_y(xp)
    got(*par_s)
    far_par_s = hidden_on(hs, q, S)
    got(x_a)
    par_a = hidden_round(ha.at[par], ha, par)
    far_own_a = hidden_on(ha, h, A)
    got(*c_yo)
    c_yo2 = cots_far_y(xo)
    for load in loads:
        load.wait()
    got(*par_a)
    far_par_a = hidden_on(ha, q, A)
    got(*c_y2, *c_ym2, *c_yp2, *c_yo2)

    def times_weight(cots, weight):
        return lax.dot_general(cots, weight, (((1,), (1,)), ((), ())), preferred_element_type=F32)

    def cots_of(hh, zd):
        return call[hh, pl.ds(zd * 2, 2)].reshape(2 * TOK, D)

    def terms_a(at, zd):
        def step(j, carry):
            units = pl.ds(pl.multiple_of(j * FT, FT), FT)
            pa[at, :, :, units] = times_weight(cots_of(h, zd), wa[units, :]).astype(BF16).reshape(2, TOK, FT)
            return carry
        lax.fori_loop(0, A // FT, step, 0)

    def terms_s(at, zd):
        def step(j, carry):
            units = pl.ds(pl.multiple_of(j * FT, FT), FT)
            both = times_weight(cots_of(h, zd), ws[units, :]) + times_weight(cots_of(q, zd), wx[units, :])
            ps[at, :, :, units] = both.astype(BF16).reshape(2, TOK, FT)
            return carry
        lax.fori_loop(0, S // FT, step, 0)

    def add(ref, at, *others):
        total = ref[at].astype(F32)
        for other, other_at in others:
            total = total + other[other_at].astype(F32)
        ref[at] = total.astype(BF16)

    everything = slice(None)

    def far(p, r2, hh, n):
        half = n // 2
        return [
            send(p.at[0, hh, :, pl.ds(0, half)], r2.at[hh, 0], to_zp),
            send(p.at[0, hh, :, pl.ds(half, half)], r2.at[hh, 1], to_zm),
        ]

    def near(p, r2, r1, hh, n):
        half = n // 2
        add(p, (1, hh, everything, slice(0, half)), (r2, (hh, 0)))
        add(p, (2, hh, everything, slice(half, n)), (r2, (hh, 1)))
        return [send(p.at[1, hh], r1.at[hh, 0], to_zp), send(p.at[2, hh], r1.at[hh, 1], to_zm)]

    def home(p, r1, hh):
        add(p, (3, hh), (r1, (hh, 0)), (r1, (hh, 1)))

    def product(ref, j, hh, part):
        hidden = ref[:, :, pl.ds(j * GT if isinstance(j, int) else pl.multiple_of(j * GT, GT), GT)].reshape(8 * TOK, GT)
        cots = call[hh, :, :, pl.ds(pl.multiple_of(part * DH, DH), DH)].reshape(8 * TOK, DH)
        out = lax.dot_general(hidden, cots, (((0,), (0,)), ((), ())), preferred_element_type=F32)
        return out.astype(BF16)

    def to_other_core(st, rv, s_sem, r_sem, j):
        return pltpu.make_async_remote_copy(
            src_ref=st.at[j], dst_ref=rv.at[j], send_sem=s_sem.at[j], recv_sem=r_sem.at[j],
            device_id=to_dp, device_id_type=MESH,
        )

    def partner_tile(j):
        xst[j] = product(hs, j, q, 1 - dp)
        to_other_core(xst, xrv, xss, xrs, j).start()
        xsum[j] = product(hs, j, q, dp)

    def own_tiles(ref, base, first, n, start=0):
        def step(j, carry):
            gst[base + j] = product(ref, j, h, 1 - dp)
            to_other_core(gst, grv, gss, grs, base + j).start()
            gw_ref[pl.ds(pl.multiple_of(first + j * GT, GT), GT), :] = product(ref, j, h, dp).astype(F32)
            return carry
        lax.fori_loop(start, n, step, 0)

    def own_sums(base, first, n):
        def step(j, carry):
            to_other_core(gst, grv, gss, grs, base + j).wait()
            gw_ref[pl.ds(pl.multiple_of(first + j * GT, GT), GT), :] += grv[base + j].astype(F32)
            return carry
        lax.fori_loop(0, n, step, 0)

    terms_a(0, zo)
    far_aq = far(pa, ra2, q, A)
    far_ah = far(pa, ra2, h, A)
    got(*far_own_s, *far_par_s)
    returns = []

    def give_back(j):
        to_other_core(xst, xrv, xss, xrs, j).wait()
        add(xsum, j, (xrv, j))
        returns.append(send(xsum.at[j], xin.at[j], to_x2))

    for j in range(NS):
        partner_tile(j)
        if j:
            give_back(j - 1)
    give_back(NS - 1)
    terms_a(1, zp)
    terms_a(2, zm)
    got(*far_aq)
    near_aq = near(pa, ra2, ra1, q, A)
    w_dp = []
    for i in range(NW):
        got(w_x[i])
        rows = pl.ds(pl.multiple_of(dp * (S // 2) + i * WR, WR), WR)
        w_dp.append(send(wx.at[rows, :], wx.at[rows, :], to_dp))
    got(*w_dp)
    terms_s(0, zo)
    far_sq = far(ps, rs2, q, S)
    far_sh = far(ps, rs2, h, S)
    terms_s(1, zp)
    terms_s(2, zm)
    got(*far_ah)
    got(*far_sq)
    near_sq = near(ps, rs2, rs1, q, S)
    near_ah = near(pa, ra2, ra1, h, A)
    got(*far_sh)
    near_sh = near(ps, rs2, rs1, h, S)
    terms_a(3, z)
    terms_s(3, z)
    got(*near_aq)
    home(pa, ra1, q)
    last_a = send(pa.at[3, q], rax, to_x2)
    got(*far_own_a, *far_par_a)
    own_tiles(hs, NA, s_own, NS)
    own_tiles(ha, 0, 0, 2)
    got(*near_sq)
    home(ps, rs1, q)
    last_s = send(ps.at[3, q], rsx, to_x2)
    own_tiles(ha, 0, 0, NA, 2)
    own_sums(0, 0, NA)
    own_sums(NA, s_own, NS)
    got(*near_ah)
    home(pa, ra1, h)
    for j in range(NS):
        got(returns[j])
        gw_ref[pl.ds(pl.multiple_of(s_other + j * GT, GT), GT), :] = xin[j].astype(F32)
    got(last_a)
    add(pa, (3, h), (rax, everything))
    gh_ref[:, 0:A] = pa[3, h]
    got(last_s)
    gh_ref[:, pl.ds(s_other, S)] = rsx[...]
    got(*near_sh)
    home(ps, rs1, h)
    gh_ref[:, pl.ds(s_own, S)] = ps[3, h]

    for copy in sent:
        copy.wait_send()


def body(hidden, cotangent, language, counts, weight):
    anywhere = pl.BlockSpec(memory_space=pl.ANY)
    vmem = pl.BlockSpec(memory_space=pltpu.VMEM)
    dma = pltpu.SemaphoreType.DMA
    return pl.pallas_call(
        kernel,
        out_shape=(pltpu.VMEM((TOK, FF), BF16), pltpu.VMEM((FF, DH), F32)),
        in_specs=[anywhere, vmem, vmem, vmem, anywhere],
        out_specs=(vmem, vmem),
        scratch_shapes=[
            pltpu.VMEM((A, D), BF16),
            pltpu.VMEM((S, D), BF16),
            pltpu.VMEM((S, D), BF16),
            pltpu.VMEM((8, TOK, A), BF16),
            pltpu.VMEM((8, TOK, S), BF16),
            pltpu.VMEM((2, 8, TOK, D), BF16),
            pltpu.VMEM((4, 2, TOK, A), BF16),
            pltpu.VMEM((4, 2, TOK, S), BF16),
            pltpu.VMEM((2, 2, TOK, A // 2), BF16),
            pltpu.VMEM((2, 2, TOK, S // 2), BF16),
            pltpu.VMEM((2, 2, TOK, A), BF16),
            pltpu.VMEM((2, 2, TOK, S), BF16),
            pltpu.VMEM((TOK, A), BF16),
            pltpu.VMEM((TOK, S), BF16),
            pltpu.VMEM((NA + NS, GT, DH), BF16),
            pltpu.VMEM((NA + NS, GT, DH), BF16),
            pltpu.VMEM((NS, GT, DH), BF16),
            pltpu.VMEM((NS, GT, DH), BF16),
            pltpu.VMEM((NS, GT, DH), BF16),
            pltpu.VMEM((NS, GT, DH), BF16),
            dma((MESSAGES,)),
            dma((MESSAGES,)),
            dma((NA + NS,)),
            dma((NA + NS,)),
            dma((NS,)),
            dma((NS,)),
            dma((4,)),
        ],
        compiler_params=pltpu.CompilerParams(
            collective_id=0, has_side_effects=True, vmem_limit_bytes=54 * 2**20
        ),
        cost_estimate=pl.CostEstimate(flops=4 * 1024 * FF * D, bytes_accessed=24 * 2**20, transcendentals=32),
    )(hidden, cotangent, language.reshape(1, TOK), counts.reshape(1, 32), weight)


def solution(mesh):
    placed = (
        P(("dp", "col"), "row"),
        P(("dp", "row"), "col"),
        P(("dp", "row")),
        P(),
        P("row", "col"),
    )
    return jax.shard_map(
        body,
        mesh=mesh,
        in_specs=placed,
        out_specs=(P(("dp", "col"), "row"), P("row", ("col", "dp"))),
        check_vma=False,
    )
```

```python
import jax
import jax.numpy as jnp
from jax import lax
from jax.experimental import pallas as pl
from jax.experimental.pallas import tpu as pltpu
from jax.sharding import PartitionSpec as P

MESH = pl.DeviceIdType.MESH
BF16 = jnp.bfloat16
F32 = jnp.float32

TOK = 128
FF = 3584
D = 1024
DH = D // 2
A = 1536
S = 1024
FT = 512
GT = 256
NA, NS = A // GT, S // GT
NW = 2
WR = S // 2 // NW
MESSAGES = 96
PIECES = 7


def column(row_vector, n):
    on_diagonal = lax.broadcasted_iota(jnp.int32, (n, n), 0) == lax.broadcasted_iota(jnp.int32, (n, n), 1)
    return jnp.sum(jnp.where(on_diagonal, jnp.broadcast_to(row_vector, (n, n)), 0.0), axis=1, keepdims=True)


def kernel(
    h_ref, c_ref, lang_ref, counts_ref, w_ref,
    gh_ref, gw_ref,
    wa, ws, wx, ha, hs, call, pa, ps, ra2, rs2, ra1, rs1, rax, rsx, gst, grv, xst, xrv, xsum, xin, lang, counts, cin,
    ss, rs, gss, grs, xss, xrs, ls,
):
    dp, row, col = lax.axis_index("dp"), lax.axis_index("row"), lax.axis_index("col")
    xl, y = row // 4, row % 4
    z, h = col // 2, col % 2
    q = 1 - h
    x = h * 2 + xl
    xp, xm, xo = (x + 1) % 4, (x + 3) % 4, (x + 2) % 4
    zp, zm, zo = (z + 1) % 4, (z + 3) % 4, (z + 2) % 4
    yp, ym, yo = (y + 1) % 4, (y + 3) % 4, (y + 2) % 4

    def device(at_x, at_y, at_z):
        return (dp, (at_x % 2) * 4 + at_y, at_z * 2 + at_x // 2)

    to_zp, to_zm = device(x, y, zp), device(x, y, zm)
    to_yp, to_ym = device(x, yp, z), device(x, ym, z)
    to_xp, to_xm, to_x2 = device(xp, y, z), device(xm, y, z), device(xo, y, z)
    to_dp = (1 - dp, row, col)
    neighbours = (to_zp, to_zm, to_yp, to_ym, to_xp, to_xm, to_x2, to_dp)

    barrier = pltpu.get_barrier_semaphore()
    for neighbour in neighbours:
        pl.semaphore_signal(barrier, inc=1, device_id=neighbour, device_id_type=MESH)

    s_own = pl.multiple_of(A + S * h, S // 2)
    s_other = pl.multiple_of(A + S * q, S // 2)
    h_a, h_s, h_o = (h_ref.at[:, pl.ds(at, n)] for at, n in ((0, A), (s_own, S), (s_other, S)))
    small = [
        pltpu.make_async_copy(lang_ref, lang, ls.at[4]),
        pltpu.make_async_copy(counts_ref, counts, ls.at[5]),
        pltpu.make_async_copy(c_ref, cin, ls.at[6]),
    ]
    loads = [
        pltpu.make_async_copy(h_a, ha.at[col], ls.at[0]),
        pltpu.make_async_copy(h_s, hs.at[col], ls.at[1]),
        pltpu.make_async_copy(w_ref.at[pl.ds(0, A), :], wa, ls.at[2]),
        pltpu.make_async_copy(w_ref.at[pl.ds(s_own, S), :], ws, ls.at[3]),
    ]
    for load in small + loads:
        load.start()
    for load in small:
        load.wait()

    lang_weight = column(jnp.sqrt(512.0 / counts[...].astype(F32)), 32)
    matches = lang[...] == lax.broadcasted_iota(jnp.int32, (32, TOK), 0)
    weight_row = jnp.sum(jnp.where(matches, lang_weight, 0.0), axis=0, keepdims=True)
    token_weight = column(weight_row, TOK)
    call[h, row] = (cin[...].astype(F32) * token_weight).astype(BF16)

    pl.semaphore_wait(barrier, len(neighbours))

    sent = []

    def send(src, dst, to):
        i = len(sent)
        copy = pltpu.make_async_remote_copy(
            src_ref=src, dst_ref=dst, send_sem=ss.at[i], recv_sem=rs.at[i], device_id=to, device_id_type=MESH
        )
        copy.start()
        sent.append(copy)
        return copy

    def got(*copies):
        for copy in copies:
            copy.wait_recv()

    def cots_whole(at_x, at_y, to):
        at = call.at[at_x // 2, (at_x % 2) * 4 + at_y]
        return send(at, at, to)

    def cots_half(at_x, at_y, half, to):
        at = call.at[at_x // 2, (at_x % 2) * 4 + at_y, pl.ds(half * (TOK // 2), TOK // 2), :]
        return send(at, at, to)

    def cots_along_y(at_x):
        return [cots_whole(at_x, y, to_yp), cots_whole(at_x, y, to_ym)]

    def cots_far_y(at_x):
        return [cots_half(at_x, ym, 0, to_yp), cots_half(at_x, yp, 1, to_ym)]

    def hidden_on(ref, hh, n):
        half = n // 2
        at_m, at_p = (ref.at[zz * 2 + hh, :, pl.ds(lo, half)] for zz, lo in ((zm, 0), (zp, half)))
        return [send(at_m, at_m, to_zp), send(at_p, at_p, to_zm)]

    def hidden_halves(ref, at, n):
        lo, hi = ref.at[at, :, pl.ds(0, n // 2)], ref.at[at, :, pl.ds(n // 2, n // 2)]
        return [send(lo, lo, to_zp), send(hi, hi, to_zm)], [send(hi, hi, to_zp), send(lo, lo, to_zm)]

    def hidden_round(src, ref, at):
        return [send(src, ref.at[at], to_zp), send(src, ref.at[at], to_zm)]

    par = z * 2 + q
    c_x = [cots_whole(x, y, to_xp), cots_whole(x, y, to_xm)]
    own_s = hidden_round(h_s, hs, col)
    c_y = cots_along_y(x)
    x_s = send(h_o, hs.at[col], to_x2)
    own_a = hidden_round(h_a, ha, col)

    got(*c_x)
    c_x2 = [cots_half(xm, y, 0, to_xp), cots_half(xp, y, 1, to_xm)]
    c_ym, c_yp = cots_along_y(xm), cots_along_y(xp)
    x_a = send(h_a, ha.at[col], to_x2)
    w_x = []
    for i in range(NW):
        rows = pl.multiple_of(dp * (S // 2) + i * WR, WR)
        w_x.append(send(w_ref.at[pl.ds(pl.multiple_of(s_other + rows, WR), WR), :], wx.at[pl.ds(rows, WR), :], to_x2))
    got(*own_s)
    far_own_s = hidden_on(hs, h, S)
    got(*c_y)
    c_y2 = cots_far_y(x)
    got(x_s)
    par_s = hidden_round(hs.at[par], hs, par)
    got(*c_x2)
    c_yo = cots_along_y(xo)
    got(*own_a)
    far_own_a = hidden_on(ha, h, A)
    got(*c_ym)
    c_ym2 = cots_far_y(xm)
    got(*c_yp)
    c_yp2 = cots_far_y(xp)
    got(*par_s)
    far_par_s = hidden_on(hs, q, S)
    got(x_a)
    par_a, par_a2 = hidden_halves(ha, par, A)
    got(*c_yo)
    c_yo2 = cots_far_y(xo)
    for load in loads:
        load.wait()
    got(*par_a)
    far_par_a = hidden_on(ha, q, A)
    got(*c_y2, *c_ym2, *c_yp2, *c_yo2)

    def times_weight(cots, weight):
        return lax.dot_general(cots, weight, (((1,), (1,)), ((), ())), preferred_element_type=F32)

    def cots_of(hh, zd):
        return call[hh, pl.ds(zd * 2, 2)].reshape(2 * TOK, D)

    def terms_a(at, zd):
        def step(j, carry):
            units = pl.ds(pl.multiple_of(j * FT, FT), FT)
            pa[at, :, :, units] = times_weight(cots_of(h, zd), wa[units, :]).astype(BF16).reshape(2, TOK, FT)
            return carry
        lax.fori_loop(0, A // FT, step, 0)

    def terms_s(at, zd):
        def step(j, carry):
            units = pl.ds(pl.multiple_of(j * FT, FT), FT)
            both = times_weight(cots_of(h, zd), ws[units, :]) + times_weight(cots_of(q, zd), wx[units, :])
            ps[at, :, :, units] = both.astype(BF16).reshape(2, TOK, FT)
            return carry
        lax.fori_loop(0, S // FT, step, 0)

    def add(ref, at, *others):
        total = ref[at].astype(F32)
        for other, other_at in others:
            total = total + other[other_at].astype(F32)
        ref[at] = total.astype(BF16)

    everything = slice(None)

    def far(p, r2, hh, n):
        half = n // 2
        return [
            send(p.at[0, hh, :, pl.ds(0, half)], r2.at[hh, 0], to_zp),
            send(p.at[0, hh, :, pl.ds(half, half)], r2.at[hh, 1], to_zm),
        ]

    def near(p, r2, r1, hh, n):
        half = n // 2
        add(p, (1, hh, everything, slice(0, half)), (r2, (hh, 0)))
        add(p, (2, hh, everything, slice(half, n)), (r2, (hh, 1)))
        return [send(p.at[1, hh], r1.at[hh, 0], to_zp), send(p.at[2, hh], r1.at[hh, 1], to_zm)]

    def home(p, r1, hh):
        add(p, (3, hh), (r1, (hh, 0)), (r1, (hh, 1)))

    def product(ref, j, hh, part):
        hidden = ref[:, :, pl.ds(j * GT if isinstance(j, int) else pl.multiple_of(j * GT, GT), GT)].reshape(8 * TOK, GT)
        cots = call[hh, :, :, pl.ds(pl.multiple_of(part * DH, DH), DH)].reshape(8 * TOK, DH)
        out = lax.dot_general(hidden, cots, (((0,), (0,)), ((), ())), preferred_element_type=F32)
        return out.astype(BF16)

    def to_other_core(st, rv, s_sem, r_sem, j):
        return pltpu.make_async_remote_copy(
            src_ref=st.at[j], dst_ref=rv.at[j], send_sem=s_sem.at[j], recv_sem=r_sem.at[j],
            device_id=to_dp, device_id_type=MESH,
        )

    def partner_tile(j):
        xst[j] = product(hs, j, q, 1 - dp)
        to_other_core(xst, xrv, xss, xrs, j).start()
        xsum[j] = product(hs, j, q, dp)

    def own_tiles(ref, base, first, n, start=0):
        def step(j, carry):
            gst[base + j] = product(ref, j, h, 1 - dp)
            to_other_core(gst, grv, gss, grs, base + j).start()
            gw_ref[pl.ds(pl.multiple_of(first + j * GT, GT), GT), :] = product(ref, j, h, dp).astype(F32)
            return carry
        lax.fori_loop(start, n, step, 0)

    def own_sums(base, first, n):
        def step(j, carry):
            to_other_core(gst, grv, gss, grs, base + j).wait()
            gw_ref[pl.ds(pl.multiple_of(first + j * GT, GT), GT), :] += grv[base + j].astype(F32)
            return carry
        lax.fori_loop(0, n, step, 0)

    terms_a(0, zo)
    far_aq = far(pa, ra2, q, A)
    far_ah = far(pa, ra2, h, A)
    got(*far_own_s, *far_par_s)
    returns = []

    def give_back(j):
        to_other_core(xst, xrv, xss, xrs, j).wait()
        add(xsum, j, (xrv, j))
        returns.append(send(xsum.at[j], xin.at[j], to_x2))

    for j in range(NS):
        partner_tile(j)
        if j:
            give_back(j - 1)
    give_back(NS - 1)
    terms_a(1, zp)
    terms_a(2, zm)
    terms_a(3, z)
    w_dp = []
    for i in range(NW):
        got(w_x[i])
        rows = pl.ds(pl.multiple_of(dp * (S // 2) + i * WR, WR), WR)
        w_dp.append(send(wx.at[rows, :], wx.at[rows, :], to_dp))
    got(*far_aq)
    near_aq = near(pa, ra2, ra1, q, A)
    got(*w_dp)
    terms_s(0, zo)
    far_sq = far(ps, rs2, q, S)
    far_sh = far(ps, rs2, h, S)
    terms_s(1, zp)
    terms_s(2, zm)
    got(*near_aq)
    home(pa, ra1, q)
    last_a = send(pa.at[3, q], rax, to_x2)
    got(*far_sq)
    near_sq = near(ps, rs2, rs1, q, S)
    got(*far_ah)
    near_ah = near(pa, ra2, ra1, h, A)
    got(*far_sh)
    near_sh = near(ps, rs2, rs1, h, S)
    terms_s(3, z)
    got(*far_own_a, *par_a2, *far_par_a)
    own_tiles(hs, NA, s_own, NS)
    own_tiles(ha, 0, 0, 2)
    got(*near_sq)
    home(ps, rs1, q)
    last_s = send(ps.at[3, q], rsx, to_x2)
    own_tiles(ha, 0, 0, NA, 2)
    own_sums(0, 0, NA)
    own_sums(NA, s_own, NS)
    got(*near_ah)
    home(pa, ra1, h)
    for j in range(NS):
        got(returns[j])
        gw_ref[pl.ds(pl.multiple_of(s_other + j * GT, GT), GT), :] = xin[j].astype(F32)
    got(last_a)
    add(pa, (3, h), (rax, everything))
    gh_ref[:, 0:A] = pa[3, h]
    got(last_s)
    gh_ref[:, pl.ds(s_other, S)] = rsx[...]
    got(*near_sh)
    home(ps, rs1, h)
    gh_ref[:, pl.ds(s_own, S)] = ps[3, h]

    for copy in sent:
        copy.wait_send()


def write_out(gh_ref, gw_ref, gh_out, gw_out, sems):
    rows = FF // PIECES
    copies = [pltpu.make_async_copy(gh_ref, gh_out, sems.at[PIECES])]
    for i in range(PIECES):
        at = pl.ds(i * rows, rows)
        copies.append(pltpu.make_async_copy(gw_ref.at[at, :], gw_out.at[at, :], sems.at[i]))
    for copy in copies:
        copy.start()
    for copy in copies:
        copy.wait()


def body(hidden, cotangent, language, counts, weight):
    anywhere = pl.BlockSpec(memory_space=pl.ANY)
    vmem = pl.BlockSpec(memory_space=pltpu.VMEM)
    dma = pltpu.SemaphoreType.DMA
    results = pl.pallas_call(
        kernel,
        out_shape=(pltpu.VMEM((TOK, FF), BF16), pltpu.VMEM((FF, DH), F32)),
        in_specs=[anywhere] * 5,
        out_specs=(vmem, vmem),
        scratch_shapes=[
            pltpu.VMEM((A, D), BF16),
            pltpu.VMEM((S, D), BF16),
            pltpu.VMEM((S, D), BF16),
            pltpu.VMEM((8, TOK, A), BF16),
            pltpu.VMEM((8, TOK, S), BF16),
            pltpu.VMEM((2, 8, TOK, D), BF16),
            pltpu.VMEM((4, 2, TOK, A), BF16),
            pltpu.VMEM((4, 2, TOK, S), BF16),
            pltpu.VMEM((2, 2, TOK, A // 2), BF16),
            pltpu.VMEM((2, 2, TOK, S // 2), BF16),
            pltpu.VMEM((2, 2, TOK, A), BF16),
            pltpu.VMEM((2, 2, TOK, S), BF16),
            pltpu.VMEM((TOK, A), BF16),
            pltpu.VMEM((TOK, S), BF16),
            pltpu.VMEM((NA + NS, GT, DH), BF16),
            pltpu.VMEM((NA + NS, GT, DH), BF16),
            pltpu.VMEM((NS, GT, DH), BF16),
            pltpu.VMEM((NS, GT, DH), BF16),
            pltpu.VMEM((NS, GT, DH), BF16),
            pltpu.VMEM((NS, GT, DH), BF16),
            pltpu.VMEM((1, TOK), jnp.int32),
            pltpu.VMEM((1, 32), jnp.int32),
            pltpu.VMEM((TOK, D), BF16),
            dma((MESSAGES,)),
            dma((MESSAGES,)),
            dma((NA + NS,)),
            dma((NA + NS,)),
            dma((NS,)),
            dma((NS,)),
            dma((7,)),
        ],
        compiler_params=pltpu.CompilerParams(
            collective_id=0, has_side_effects=True, vmem_limit_bytes=54 * 2**20
        ),
        cost_estimate=pl.CostEstimate(flops=4 * 1024 * FF * D, bytes_accessed=24 * 2**20, transcendentals=32),
    )(hidden, cotangent, language.reshape(1, TOK), counts.reshape(1, 32), weight)
    return pl.pallas_call(
        write_out,
        out_shape=(jax.ShapeDtypeStruct((TOK, FF), BF16), jax.ShapeDtypeStruct((FF, DH), F32)),
        in_specs=[vmem, vmem],
        out_specs=(anywhere, anywhere),
        scratch_shapes=[dma((PIECES + 1,))],
        compiler_params=pltpu.CompilerParams(vmem_limit_bytes=2**20),
    )(*results)


def solution(mesh):
    placed = (
        P(("dp", "col"), "row"),
        P(("dp", "row"), "col"),
        P(("dp", "row")),
        P(),
        P("row", "col"),
    )
    return jax.shard_map(
        body,
        mesh=mesh,
        in_specs=placed,
        out_specs=(P(("dp", "col"), "row"), P("row", ("col", "dp"))),
        check_vma=False,
    )
```

```python
import jax
import jax.numpy as jnp
from jax import lax
from jax.experimental import pallas as pl
from jax.experimental.pallas import tpu as pltpu
from jax.sharding import PartitionSpec as P

MESH = pl.DeviceIdType.MESH
BF16 = jnp.bfloat16
F32 = jnp.float32

TOK = 128
FF = 3584
D = 1024
DH = D // 2
A, S = 1536, 1024
AW, SW = 1280, 1152
FT = 512
TA, TS = 256, 384
NA, NS = AW // TA, SW // TS
NW = 2
WR = S // 2 // NW
MESSAGES = 96
PIECES = 7


def column(row_vector, n):
    on_diagonal = lax.broadcasted_iota(jnp.int32, (n, n), 0) == lax.broadcasted_iota(jnp.int32, (n, n), 1)
    return jnp.sum(jnp.where(on_diagonal, jnp.broadcast_to(row_vector, (n, n)), 0.0), axis=1, keepdims=True)


def kernel(
    h_ref, c_ref, lang_ref, counts_ref, w_ref,
    gh_ref, gw_ref,
    wa, ws, wx, ha, hs, call, pa, ps, ra2, rs2, ra1, rs1, rax, rsx, gsa, gra, gss, grs, xst, xrv, xsum, xin, lang, counts, cin,
    ss, rs, sem_a, sem_s, sem_x, ls,
):
    dp, row, col = lax.axis_index("dp"), lax.axis_index("row"), lax.axis_index("col")
    xl, y = row // 4, row % 4
    z, h = col // 2, col % 2
    q = 1 - h
    x = h * 2 + xl
    xp, xm, xo = (x + 1) % 4, (x + 3) % 4, (x + 2) % 4
    zp, zm, zo = (z + 1) % 4, (z + 3) % 4, (z + 2) % 4
    yp, ym, yo = (y + 1) % 4, (y + 3) % 4, (y + 2) % 4

    def device(at_x, at_y, at_z):
        return (dp, (at_x % 2) * 4 + at_y, at_z * 2 + at_x // 2)

    to_zp, to_zm = device(x, y, zp), device(x, y, zm)
    to_yp, to_ym = device(x, yp, z), device(x, ym, z)
    to_xp, to_xm, to_x2 = device(xp, y, z), device(xm, y, z), device(xo, y, z)
    to_dp = (1 - dp, row, col)
    neighbours = (to_zp, to_zm, to_yp, to_ym, to_xp, to_xm, to_x2, to_dp)

    barrier = pltpu.get_barrier_semaphore()
    for neighbour in neighbours:
        pl.semaphore_signal(barrier, inc=1, device_id=neighbour, device_id_type=MESH)

    s_own = pl.multiple_of(A + S * h, S // 2)
    s_other = pl.multiple_of(A + S * q, S // 2)
    sw_own = pl.multiple_of(AW + SW * h, 128)
    sw_other = pl.multiple_of(AW + SW * q, 128)
    h_a, h_s, h_o = (h_ref.at[:, pl.ds(at, n)] for at, n in ((0, AW), (sw_own, SW), (sw_other, SW)))
    small = [
        pltpu.make_async_copy(lang_ref, lang, ls.at[4]),
        pltpu.make_async_copy(counts_ref, counts, ls.at[5]),
        pltpu.make_async_copy(c_ref, cin, ls.at[6]),
    ]
    loads = [
        pltpu.make_async_copy(h_a, ha.at[col], ls.at[0]),
        pltpu.make_async_copy(h_s, hs.at[col], ls.at[1]),
        pltpu.make_async_copy(w_ref.at[pl.ds(0, A), :], wa, ls.at[2]),
        pltpu.make_async_copy(w_ref.at[pl.ds(s_own, S), :], ws, ls.at[3]),
    ]
    for load in small + loads:
        load.start()
    for load in small:
        load.wait()

    lang_weight = column(jnp.sqrt(512.0 / counts[...].astype(F32)), 32)
    matches = lang[...] == lax.broadcasted_iota(jnp.int32, (32, TOK), 0)
    weight_row = jnp.sum(jnp.where(matches, lang_weight, 0.0), axis=0, keepdims=True)
    token_weight = column(weight_row, TOK)
    call[h, row] = (cin[...].astype(F32) * token_weight).astype(BF16)

    pl.semaphore_wait(barrier, len(neighbours))

    sent = []

    def send(src, dst, to):
        i = len(sent)
        copy = pltpu.make_async_remote_copy(
            src_ref=src, dst_ref=dst, send_sem=ss.at[i], recv_sem=rs.at[i], device_id=to, device_id_type=MESH
        )
        copy.start()
        sent.append(copy)
        return copy

    def got(*copies):
        for copy in copies:
            copy.wait_recv()

    def cots_whole(at_x, at_y, to):
        at = call.at[at_x // 2, (at_x % 2) * 4 + at_y]
        return send(at, at, to)

    def cots_half(at_x, at_y, half, to):
        at = call.at[at_x // 2, (at_x % 2) * 4 + at_y, pl.ds(half * (TOK // 2), TOK // 2), :]
        return send(at, at, to)

    def cots_along_y(at_x):
        return [cots_whole(at_x, y, to_yp), cots_whole(at_x, y, to_ym)]

    def cots_far_y(at_x):
        return [cots_half(at_x, ym, 0, to_yp), cots_half(at_x, yp, 1, to_ym)]

    def hidden_on(ref, hh, n, cut):
        at_m, at_p = ref.at[zm * 2 + hh, :, pl.ds(0, cut)], ref.at[zp * 2 + hh, :, pl.ds(cut, n - cut)]
        return [send(at_m, at_m, to_zp), send(at_p, at_p, to_zm)]

    def hidden_halves(ref, at, n):
        lo, hi = ref.at[at, :, pl.ds(0, n // 2)], ref.at[at, :, pl.ds(n // 2, n // 2)]
        return [send(lo, lo, to_zp), send(hi, hi, to_zm)], [send(hi, hi, to_zp), send(lo, lo, to_zm)]

    def hidden_round(src, ref, at):
        return [send(src, ref.at[at], to_zp), send(src, ref.at[at], to_zm)]

    par = z * 2 + q
    c_x = [cots_whole(x, y, to_xp), cots_whole(x, y, to_xm)]
    own_s = hidden_round(h_s, hs, col)
    c_y = cots_along_y(x)
    x_s = send(h_o, hs.at[col], to_x2)
    own_a = hidden_round(h_a, ha, col)

    got(*c_x)
    c_x2 = [cots_half(xm, y, 0, to_xp), cots_half(xp, y, 1, to_xm)]
    c_ym, c_yp = cots_along_y(xm), cots_along_y(xp)
    x_a = send(h_a, ha.at[col], to_x2)
    w_x = []
    for i in range(NW):
        rows = pl.multiple_of(dp * (S // 2) + i * WR, WR)
        w_x.append(send(w_ref.at[pl.ds(pl.multiple_of(s_other + rows, WR), WR), :], wx.at[pl.ds(rows, WR), :], to_x2))
    got(*own_s)
    far_own_s = hidden_on(hs, h, SW, 640)
    got(*c_y)
    c_y2 = cots_far_y(x)
    got(x_s)
    par_s = hidden_round(hs.at[par], hs, par)
    got(*c_x2)
    c_yo = cots_along_y(xo)
    got(*own_a)
    far_own_a = hidden_on(ha, h, AW, AW // 2)
    got(*c_ym)
    c_ym2 = cots_far_y(xm)
    got(*c_yp)
    c_yp2 = cots_far_y(xp)
    got(*par_s)
    far_par_s = hidden_on(hs, q, SW, 512)
    got(x_a)
    par_a, par_a2 = hidden_halves(ha, par, AW)
    got(*c_yo)
    c_yo2 = cots_far_y(xo)
    for load in loads:
        load.wait()
    got(*par_a)
    far_par_a = hidden_on(ha, q, AW, AW // 2)
    got(*c_y2, *c_ym2, *c_yp2, *c_yo2)

    def times_weight(cots, weight):
        return lax.dot_general(cots, weight, (((1,), (1,)), ((), ())), preferred_element_type=F32)

    def cots_of(hh, zd):
        return call[hh, pl.ds(zd * 2, 2)].reshape(2 * TOK, D)

    def terms_a(at, zd):
        def step(j, carry):
            units = pl.ds(pl.multiple_of(j * FT, FT), FT)
            pa[at, :, :, units] = times_weight(cots_of(h, zd), wa[units, :]).astype(BF16).reshape(2, TOK, FT)
            return carry
        lax.fori_loop(0, A // FT, step, 0)

    def terms_s(at, zd):
        def step(j, carry):
            units = pl.ds(pl.multiple_of(j * FT, FT), FT)
            both = times_weight(cots_of(h, zd), ws[units, :]) + times_weight(cots_of(q, zd), wx[units, :])
            ps[at, :, :, units] = both.astype(BF16).reshape(2, TOK, FT)
            return carry
        lax.fori_loop(0, S // FT, step, 0)

    def add(ref, at, *others):
        total = ref[at].astype(F32)
        for other, other_at in others:
            total = total + other[other_at].astype(F32)
        ref[at] = total.astype(BF16)

    everything = slice(None)

    def far(p, r2, hh, n):
        half = n // 2
        return [
            send(p.at[0, hh, :, pl.ds(0, half)], r2.at[hh, 0], to_zp),
            send(p.at[0, hh, :, pl.ds(half, half)], r2.at[hh, 1], to_zm),
        ]

    def near(p, r2, r1, hh, n):
        half = n // 2
        add(p, (1, hh, everything, slice(0, half)), (r2, (hh, 0)))
        add(p, (2, hh, everything, slice(half, n)), (r2, (hh, 1)))
        return [send(p.at[1, hh], r1.at[hh, 0], to_zp), send(p.at[2, hh], r1.at[hh, 1], to_zm)]

    def home(p, r1, hh):
        add(p, (3, hh), (r1, (hh, 0)), (r1, (hh, 1)))

    def product(ref, units, hh, part):
        hidden = ref[:, :, units].reshape(8 * TOK, units.size)
        cots = call[hh, :, :, pl.ds(pl.multiple_of(part * DH, DH), DH)].reshape(8 * TOK, DH)
        out = lax.dot_general(hidden, cots, (((0,), (0,)), ((), ())), preferred_element_type=F32)
        return out.astype(BF16)

    def to_other_core(st, rv, sems, j):
        return pltpu.make_async_remote_copy(
            src_ref=st.at[j], dst_ref=rv.at[j], send_sem=sems.at[0, j], recv_sem=sems.at[1, j],
            device_id=to_dp, device_id_type=MESH,
        )

    def partner_tile(j):
        units = pl.ds(j * TS, TS)
        xst[j] = product(hs, units, q, 1 - dp)
        to_other_core(xst, xrv, sem_x, j).start()
        xsum[j] = product(hs, units, q, dp)

    def own_tiles(ref, st, rv, sems, size, first, lo, hi):
        def step(j, carry):
            units = pl.ds(pl.multiple_of(j * size, 128), size)
            st[j] = product(ref, units, h, 1 - dp)
            to_other_core(st, rv, sems, j).start()
            gw_ref[pl.ds(pl.multiple_of(first + j * size, 128), size), :] = product(ref, units, h, dp).astype(F32)
            return carry
        lax.fori_loop(lo, hi, step, 0)

    def own_sums(st, rv, sems, size, first, n):
        def step(j, carry):
            to_other_core(st, rv, sems, j).wait()
            gw_ref[pl.ds(pl.multiple_of(first + j * size, 128), size), :] += rv[j].astype(F32)
            return carry
        lax.fori_loop(0, n, step, 0)

    terms_a(0, zo)
    far_aq = far(pa, ra2, q, A)
    far_ah = far(pa, ra2, h, A)
    got(*far_own_s, *far_par_s)
    returns = []

    def give_back(j):
        to_other_core(xst, xrv, sem_x, j).wait()
        add(xsum, j, (xrv, j))
        returns.append(send(xsum.at[j], xin.at[j], to_x2))

    for j in range(NS):
        partner_tile(j)
        if j:
            give_back(j - 1)
    give_back(NS - 1)
    terms_a(1, zp)
    terms_a(2, zm)
    terms_a(3, z)
    w_dp = []
    for i in range(NW):
        got(w_x[i])
        rows = pl.ds(pl.multiple_of(dp * (S // 2) + i * WR, WR), WR)
        w_dp.append(send(wx.at[rows, :], wx.at[rows, :], to_dp))
    got(*far_aq)
    near_aq = near(pa, ra2, ra1, q, A)
    got(*w_dp)
    terms_s(0, zo)
    far_sq = far(ps, rs2, q, S)
    far_sh = far(ps, rs2, h, S)
    terms_s(1, zp)
    terms_s(2, zm)
    got(*near_aq)
    home(pa, ra1, q)
    last_a = send(pa.at[3, q], rax, to_x2)
    got(*far_sq)
    near_sq = near(ps, rs2, rs1, q, S)
    got(*far_ah)
    near_ah = near(pa, ra2, ra1, h, A)
    got(*far_sh)
    near_sh = near(ps, rs2, rs1, h, S)
    terms_s(3, z)
    got(*far_own_a, *par_a2, *far_par_a)
    own_tiles(hs, gss, grs, sem_s, TS, sw_own, 0, NS)
    own_tiles(ha, gsa, gra, sem_a, TA, 0, 0, 1)
    got(*near_sq)
    home(ps, rs1, q)
    last_s = send(ps.at[3, q], rsx, to_x2)
    own_tiles(ha, gsa, gra, sem_a, TA, 0, 1, NA)
    own_sums(gsa, gra, sem_a, TA, 0, NA)
    own_sums(gss, grs, sem_s, TS, sw_own, NS)
    got(*near_ah)
    home(pa, ra1, h)
    for j in range(NS):
        got(returns[j])
        gw_ref[pl.ds(pl.multiple_of(sw_other + j * TS, 128), TS), :] = xin[j].astype(F32)
    got(last_a)
    add(pa, (3, h), (rax, everything))
    gh_ref[:, 0:A] = pa[3, h]
    got(last_s)
    gh_ref[:, pl.ds(s_other, S)] = rsx[...]
    got(*near_sh)
    home(ps, rs1, h)
    gh_ref[:, pl.ds(s_own, S)] = ps[3, h]

    for copy in sent:
        copy.wait_send()


def write_out(gh_ref, gw_ref, gh_out, gw_out, sems):
    rows = FF // PIECES
    copies = [pltpu.make_async_copy(gh_ref, gh_out, sems.at[PIECES])]
    for i in range(PIECES):
        at = pl.ds(i * rows, rows)
        copies.append(pltpu.make_async_copy(gw_ref.at[at, :], gw_out.at[at, :], sems.at[i]))
    for copy in copies:
        copy.start()
    for copy in copies:
        copy.wait()


def body(hidden, cotangent, language, counts, weight):
    anywhere = pl.BlockSpec(memory_space=pl.ANY)
    vmem = pl.BlockSpec(memory_space=pltpu.VMEM)
    dma = pltpu.SemaphoreType.DMA
    results = pl.pallas_call(
        kernel,
        out_shape=(pltpu.VMEM((TOK, FF), BF16), pltpu.VMEM((FF, DH), F32)),
        in_specs=[anywhere] * 5,
        out_specs=(vmem, vmem),
        scratch_shapes=[
            pltpu.VMEM((A, D), BF16),
            pltpu.VMEM((S, D), BF16),
            pltpu.VMEM((S, D), BF16),
            pltpu.VMEM((8, TOK, AW), BF16),
            pltpu.VMEM((8, TOK, SW), BF16),
            pltpu.VMEM((2, 8, TOK, D), BF16),
            pltpu.VMEM((4, 2, TOK, A), BF16),
            pltpu.VMEM((4, 2, TOK, S), BF16),
            pltpu.VMEM((2, 2, TOK, A // 2), BF16),
            pltpu.VMEM((2, 2, TOK, S // 2), BF16),
            pltpu.VMEM((2, 2, TOK, A), BF16),
            pltpu.VMEM((2, 2, TOK, S), BF16),
            pltpu.VMEM((TOK, A), BF16),
            pltpu.VMEM((TOK, S), BF16),
            pltpu.VMEM((NA, TA, DH), BF16),
            pltpu.VMEM((NA, TA, DH), BF16),
            pltpu.VMEM((NS, TS, DH), BF16),
            pltpu.VMEM((NS, TS, DH), BF16),
            pltpu.VMEM((NS, TS, DH), BF16),
            pltpu.VMEM((NS, TS, DH), BF16),
            pltpu.VMEM((NS, TS, DH), BF16),
            pltpu.VMEM((NS, TS, DH), BF16),
            pltpu.VMEM((1, TOK), jnp.int32),
            pltpu.VMEM((1, 32), jnp.int32),
            pltpu.VMEM((TOK, D), BF16),
            dma((MESSAGES,)),
            dma((MESSAGES,)),
            dma((2, NA)),
            dma((2, NS)),
            dma((2, NS)),
            dma((7,)),
        ],
        compiler_params=pltpu.CompilerParams(
            collective_id=0, has_side_effects=True, vmem_limit_bytes=54 * 2**20
        ),
        cost_estimate=pl.CostEstimate(flops=4 * 1024 * FF * D, bytes_accessed=24 * 2**20, transcendentals=32),
    )(hidden, cotangent, language.reshape(1, TOK), counts.reshape(1, 32), weight)
    return pl.pallas_call(
        write_out,
        out_shape=(jax.ShapeDtypeStruct((TOK, FF), BF16), jax.ShapeDtypeStruct((FF, DH), F32)),
        in_specs=[vmem, vmem],
        out_specs=(anywhere, anywhere),
        scratch_shapes=[dma((PIECES + 1,))],
        compiler_params=pltpu.CompilerParams(vmem_limit_bytes=2**20),
    )(*results)


def solution(mesh):
    placed = (
        P(("dp", "col"), "row"),
        P(("dp", "row"), "col"),
        P(("dp", "row")),
        P(),
        P("row", "col"),
    )
    return jax.shard_map(
        body,
        mesh=mesh,
        in_specs=placed,
        out_specs=(P(("dp", "col"), "row"), P("row", ("col", "dp"))),
        check_vma=False,
    )
```

```python
import jax
import jax.numpy as jnp
from jax import lax
from jax.experimental import pallas as pl
from jax.experimental.pallas import tpu as pltpu
from jax.sharding import PartitionSpec as P

MESH = pl.DeviceIdType.MESH
BF16 = jnp.bfloat16
F32 = jnp.float32

TOK = 128
FF = 3584
D = 1024
DH = D // 2
A, S = 1536, 1024
AW, SW = 1280, 1152
FT = 512
TA, TS = 256, 384
NA, NS = AW // TA, SW // TS
NW = 4
WR = S // 2 // NW
MESSAGES = 96
PIECES = 7


def column(row_vector, n):
    on_diagonal = lax.broadcasted_iota(jnp.int32, (n, n), 0) == lax.broadcasted_iota(jnp.int32, (n, n), 1)
    return jnp.sum(jnp.where(on_diagonal, jnp.broadcast_to(row_vector, (n, n)), 0.0), axis=1, keepdims=True)


def kernel(
    h_ref, c_ref, lang_ref, counts_ref, w_ref,
    gh_ref, gw_ref,
    wa, ws, wx, ha, hs, call, pa, ps, ra2, rs2, ra1, rs1, rax, rsx, gsa, gra, gss, grs, xst, xrv, xsum, xin, lang, counts, cin,
    ss, rs, sem_a, sem_s, sem_x, ls,
):
    dp, row, col = lax.axis_index("dp"), lax.axis_index("row"), lax.axis_index("col")
    xl, y = row // 4, row % 4
    z, h = col // 2, col % 2
    q = 1 - h
    x = h * 2 + xl
    xp, xm, xo = (x + 1) % 4, (x + 3) % 4, (x + 2) % 4
    zp, zm, zo = (z + 1) % 4, (z + 3) % 4, (z + 2) % 4
    yp, ym, yo = (y + 1) % 4, (y + 3) % 4, (y + 2) % 4

    def device(at_x, at_y, at_z):
        return (dp, (at_x % 2) * 4 + at_y, at_z * 2 + at_x // 2)

    to_zp, to_zm = device(x, y, zp), device(x, y, zm)
    to_yp, to_ym = device(x, yp, z), device(x, ym, z)
    to_xp, to_xm, to_x2 = device(xp, y, z), device(xm, y, z), device(xo, y, z)
    to_dp = (1 - dp, row, col)
    neighbours = (to_zp, to_zm, to_yp, to_ym, to_xp, to_xm, to_x2, to_dp)

    barrier = pltpu.get_barrier_semaphore()
    for neighbour in neighbours:
        pl.semaphore_signal(barrier, inc=1, device_id=neighbour, device_id_type=MESH)

    s_own = pl.multiple_of(A + S * h, S // 2)
    s_other = pl.multiple_of(A + S * q, S // 2)
    sw_own = pl.multiple_of(AW + SW * h, 128)
    sw_other = pl.multiple_of(AW + SW * q, 128)
    h_a, h_s, h_o = (h_ref.at[:, pl.ds(at, n)] for at, n in ((0, AW), (sw_own, SW), (sw_other, SW)))
    small = [
        pltpu.make_async_copy(lang_ref, lang, ls.at[4]),
        pltpu.make_async_copy(counts_ref, counts, ls.at[5]),
        pltpu.make_async_copy(c_ref, cin, ls.at[6]),
    ]
    loads = [
        pltpu.make_async_copy(h_a, ha.at[col], ls.at[0]),
        pltpu.make_async_copy(h_s, hs.at[col], ls.at[1]),
        pltpu.make_async_copy(w_ref.at[pl.ds(0, A), :], wa, ls.at[2]),
        pltpu.make_async_copy(w_ref.at[pl.ds(s_own, S), :], ws, ls.at[3]),
    ]
    for load in small + loads:
        load.start()
    for load in small:
        load.wait()

    lang_weight = column(jnp.sqrt(512.0 / counts[...].astype(F32)), 32)
    matches = lang[...] == lax.broadcasted_iota(jnp.int32, (32, TOK), 0)
    weight_row = jnp.sum(jnp.where(matches, lang_weight, 0.0), axis=0, keepdims=True)
    token_weight = column(weight_row, TOK)
    call[h, row] = (cin[...].astype(F32) * token_weight).astype(BF16)

    pl.semaphore_wait(barrier, len(neighbours))

    sent = []

    def send(src, dst, to):
        i = len(sent)
        copy = pltpu.make_async_remote_copy(
            src_ref=src, dst_ref=dst, send_sem=ss.at[i], recv_sem=rs.at[i], device_id=to, device_id_type=MESH
        )
        copy.start()
        sent.append(copy)
        return copy

    def got(*copies):
        for copy in copies:
            copy.wait_recv()

    def cots_whole(at_x, at_y, to):
        at = call.at[at_x // 2, (at_x % 2) * 4 + at_y]
        return send(at, at, to)

    def cots_half(at_x, at_y, half, to):
        at = call.at[at_x // 2, (at_x % 2) * 4 + at_y, pl.ds(half * (TOK // 2), TOK // 2), :]
        return send(at, at, to)

    def cots_along_y(at_x):
        return [cots_whole(at_x, y, to_yp), cots_whole(at_x, y, to_ym)]

    def cots_far_y(at_x):
        return [cots_half(at_x, ym, 0, to_yp), cots_half(at_x, yp, 1, to_ym)]

    def hidden_on(ref, hh, n, cut):
        at_m, at_p = ref.at[zm * 2 + hh, :, pl.ds(0, cut)], ref.at[zp * 2 + hh, :, pl.ds(cut, n - cut)]
        return [send(at_m, at_m, to_zp), send(at_p, at_p, to_zm)]

    def hidden_halves(ref, at, n):
        lo, hi = ref.at[at, :, pl.ds(0, n // 2)], ref.at[at, :, pl.ds(n // 2, n // 2)]
        return [send(lo, lo, to_zp), send(hi, hi, to_zm)], [send(hi, hi, to_zp), send(lo, lo, to_zm)]

    def hidden_round(src, ref, at):
        return [send(src, ref.at[at], to_zp), send(src, ref.at[at], to_zm)]

    par = z * 2 + q
    c_x = [cots_whole(x, y, to_xp), cots_whole(x, y, to_xm)]
    own_s = hidden_round(h_s, hs, col)
    c_y = cots_along_y(x)
    x_s = send(h_o, hs.at[col], to_x2)
    own_a = hidden_round(h_a, ha, col)

    got(*c_x)
    c_x2 = [cots_half(xm, y, 0, to_xp), cots_half(xp, y, 1, to_xm)]
    c_ym, c_yp = cots_along_y(xm), cots_along_y(xp)
    x_a = send(h_a, ha.at[col], to_x2)
    w_x = []
    for i in range(NW):
        rows = pl.multiple_of(dp * (S // 2) + i * WR, WR)
        w_x.append(send(w_ref.at[pl.ds(pl.multiple_of(s_other + rows, WR), WR), :], wx.at[pl.ds(rows, WR), :], to_x2))
    got(*own_s)
    far_own_s = hidden_on(hs, h, SW, 640)
    got(*c_y)
    c_y2 = cots_far_y(x)
    got(x_s)
    par_s = hidden_round(hs.at[par], hs, par)
    got(*c_x2)
    c_yo = cots_along_y(xo)
    got(*own_a)
    far_own_a = hidden_on(ha, h, AW, AW // 2)
    got(*c_ym)
    c_ym2 = cots_far_y(xm)
    got(*c_yp)
    c_yp2 = cots_far_y(xp)
    got(*par_s)
    far_par_s = hidden_on(hs, q, SW, 512)
    got(x_a)
    par_a, par_a2 = hidden_halves(ha, par, AW)
    got(*c_yo)
    c_yo2 = cots_far_y(xo)
    for load in loads:
        load.wait()
    got(*par_a)
    far_par_a = hidden_on(ha, q, AW, AW // 2)
    got(*c_y2, *c_ym2, *c_yp2, *c_yo2)

    def times_weight(cots, weight):
        return lax.dot_general(cots, weight, (((1,), (1,)), ((), ())), preferred_element_type=F32)

    def cots_of(hh, zd):
        return call[hh, pl.ds(zd * 2, 2)].reshape(2 * TOK, D)

    def terms_a(at, zd):
        def step(j, carry):
            units = pl.ds(pl.multiple_of(j * FT, FT), FT)
            pa[at, :, :, units] = times_weight(cots_of(h, zd), wa[units, :]).astype(BF16).reshape(2, TOK, FT)
            return carry
        lax.fori_loop(0, A // FT, step, 0)

    def terms_s(at, zd):
        def step(j, carry):
            units = pl.ds(pl.multiple_of(j * FT, FT), FT)
            both = times_weight(cots_of(h, zd), ws[units, :]) + times_weight(cots_of(q, zd), wx[units, :])
            ps[at, :, :, units] = both.astype(BF16).reshape(2, TOK, FT)
            return carry
        lax.fori_loop(0, S // FT, step, 0)

    def add(ref, at, *others):
        total = ref[at].astype(F32)
        for other, other_at in others:
            total = total + other[other_at].astype(F32)
        ref[at] = total.astype(BF16)

    everything = slice(None)

    def far(p, r2, hh, n):
        half = n // 2
        return [
            send(p.at[0, hh, :, pl.ds(0, half)], r2.at[hh, 0], to_zp),
            send(p.at[0, hh, :, pl.ds(half, half)], r2.at[hh, 1], to_zm),
        ]

    def near(p, r2, r1, hh, n):
        half = n // 2
        add(p, (1, hh, everything, slice(0, half)), (r2, (hh, 0)))
        add(p, (2, hh, everything, slice(half, n)), (r2, (hh, 1)))
        return [send(p.at[1, hh], r1.at[hh, 0], to_zp), send(p.at[2, hh], r1.at[hh, 1], to_zm)]

    def home(p, r1, hh):
        add(p, (3, hh), (r1, (hh, 0)), (r1, (hh, 1)))

    def product(ref, units, hh, part):
        hidden = ref[:, :, units].reshape(8 * TOK, units.size)
        cots = call[hh, :, :, pl.ds(pl.multiple_of(part * DH, DH), DH)].reshape(8 * TOK, DH)
        out = lax.dot_general(hidden, cots, (((0,), (0,)), ((), ())), preferred_element_type=F32)
        return out.astype(BF16)

    def to_other_core(st, rv, sems, j):
        return pltpu.make_async_remote_copy(
            src_ref=st.at[j], dst_ref=rv.at[j], send_sem=sems.at[0, j], recv_sem=sems.at[1, j],
            device_id=to_dp, device_id_type=MESH,
        )

    def partner_tile(j):
        units = pl.ds(j * TS, TS)
        xst[j] = product(hs, units, q, 1 - dp)
        to_other_core(xst, xrv, sem_x, j).start()
        xsum[j] = product(hs, units, q, dp)

    def own_tiles(ref, st, rv, sems, size, first, lo, hi):
        def step(j, carry):
            units = pl.ds(pl.multiple_of(j * size, 128), size)
            st[j] = product(ref, units, h, 1 - dp)
            to_other_core(st, rv, sems, j).start()
            gw_ref[pl.ds(pl.multiple_of(first + j * size, 128), size), :] = product(ref, units, h, dp).astype(F32)
            return carry
        lax.fori_loop(lo, hi, step, 0)

    def own_sums(st, rv, sems, size, first, n):
        def step(j, carry):
            to_other_core(st, rv, sems, j).wait()
            gw_ref[pl.ds(pl.multiple_of(first + j * size, 128), size), :] += rv[j].astype(F32)
            return carry
        lax.fori_loop(0, n, step, 0)

    terms_a(0, zo)
    far_aq = far(pa, ra2, q, A)
    far_ah = far(pa, ra2, h, A)
    got(*far_own_s, *far_par_s)
    returns = []

    def give_back(j):
        to_other_core(xst, xrv, sem_x, j).wait()
        add(xsum, j, (xrv, j))
        returns.append(send(xsum.at[j], xin.at[j], to_x2))

    for j in range(NS):
        partner_tile(j)
        if j:
            give_back(j - 1)
    give_back(NS - 1)
    terms_a(1, zp)
    terms_a(2, zm)
    w_dp = []
    for i in range(NW):
        got(w_x[i])
        rows = pl.ds(pl.multiple_of(dp * (S // 2) + i * WR, WR), WR)
        w_dp.append(send(wx.at[rows, :], wx.at[rows, :], to_dp))
    got(*far_aq)
    near_aq = near(pa, ra2, ra1, q, A)
    terms_a(3, z)
    got(*w_dp)
    terms_s(0, zo)
    far_sq = far(ps, rs2, q, S)
    far_sh = far(ps, rs2, h, S)
    terms_s(1, zp)
    terms_s(2, zm)
    got(*near_aq)
    home(pa, ra1, q)
    last_a = send(pa.at[3, q], rax, to_x2)
    got(*far_sq)
    near_sq = near(ps, rs2, rs1, q, S)
    got(*far_ah)
    near_ah = near(pa, ra2, ra1, h, A)
    got(*far_sh)
    near_sh = near(ps, rs2, rs1, h, S)
    terms_s(3, z)
    got(*far_own_a, *par_a2, *far_par_a)
    own_tiles(hs, gss, grs, sem_s, TS, sw_own, 0, NS)
    own_tiles(ha, gsa, gra, sem_a, TA, 0, 0, 1)
    got(*near_sq)
    home(ps, rs1, q)
    last_s = send(ps.at[3, q], gh_ref.at[:, pl.ds(s_own, S)], to_x2)
    own_tiles(ha, gsa, gra, sem_a, TA, 0, 1, NA)
    own_sums(gsa, gra, sem_a, TA, 0, NA)
    own_sums(gss, grs, sem_s, TS, sw_own, NS)
    got(*near_ah)
    home(pa, ra1, h)
    for j in range(NS):
        got(returns[j])
        gw_ref[pl.ds(pl.multiple_of(sw_other + j * TS, 128), TS), :] = xin[j].astype(F32)
    got(last_a)
    add(pa, (3, h), (rax, everything))
    gh_ref[:, 0:A] = pa[3, h]
    got(*near_sh)
    home(ps, rs1, h)
    gh_ref[:, pl.ds(s_own, S)] = ps[3, h]
    got(last_s)

    for copy in sent:
        copy.wait_send()


def write_out(gh_ref, gw_ref, gh_out, gw_out, sems):
    rows = FF // PIECES
    copies = [pltpu.make_async_copy(gh_ref, gh_out, sems.at[PIECES])]
    for i in range(PIECES):
        at = pl.ds(i * rows, rows)
        copies.append(pltpu.make_async_copy(gw_ref.at[at, :], gw_out.at[at, :], sems.at[i]))
    for copy in copies:
        copy.start()
    for copy in copies:
        copy.wait()


def body(hidden, cotangent, language, counts, weight):
    anywhere = pl.BlockSpec(memory_space=pl.ANY)
    vmem = pl.BlockSpec(memory_space=pltpu.VMEM)
    dma = pltpu.SemaphoreType.DMA
    results = pl.pallas_call(
        kernel,
        out_shape=(pltpu.VMEM((TOK, FF), BF16), pltpu.VMEM((FF, DH), F32)),
        in_specs=[anywhere] * 5,
        out_specs=(vmem, vmem),
        scratch_shapes=[
            pltpu.VMEM((A, D), BF16),
            pltpu.VMEM((S, D), BF16),
            pltpu.VMEM((S, D), BF16),
            pltpu.VMEM((8, TOK, AW), BF16),
            pltpu.VMEM((8, TOK, SW), BF16),
            pltpu.VMEM((2, 8, TOK, D), BF16),
            pltpu.VMEM((4, 2, TOK, A), BF16),
            pltpu.VMEM((4, 2, TOK, S), BF16),
            pltpu.VMEM((2, 2, TOK, A // 2), BF16),
            pltpu.VMEM((2, 2, TOK, S // 2), BF16),
            pltpu.VMEM((2, 2, TOK, A), BF16),
            pltpu.VMEM((2, 2, TOK, S), BF16),
            pltpu.VMEM((TOK, A), BF16),
            pltpu.VMEM((TOK, S), BF16),
            pltpu.VMEM((NA, TA, DH), BF16),
            pltpu.VMEM((NA, TA, DH), BF16),
            pltpu.VMEM((NS, TS, DH), BF16),
            pltpu.VMEM((NS, TS, DH), BF16),
            pltpu.VMEM((NS, TS, DH), BF16),
            pltpu.VMEM((NS, TS, DH), BF16),
            pltpu.VMEM((NS, TS, DH), BF16),
            pltpu.VMEM((NS, TS, DH), BF16),
            pltpu.VMEM((1, TOK), jnp.int32),
            pltpu.VMEM((1, 32), jnp.int32),
            pltpu.VMEM((TOK, D), BF16),
            dma((MESSAGES,)),
            dma((MESSAGES,)),
            dma((2, NA)),
            dma((2, NS)),
            dma((2, NS)),
            dma((7,)),
        ],
        compiler_params=pltpu.CompilerParams(
            collective_id=0, has_side_effects=True, vmem_limit_bytes=54 * 2**20
        ),
        cost_estimate=pl.CostEstimate(flops=4 * 1024 * FF * D, bytes_accessed=24 * 2**20, transcendentals=32),
    )(hidden, cotangent, language.reshape(1, TOK), counts.reshape(1, 32), weight)
    return pl.pallas_call(
        write_out,
        out_shape=(jax.ShapeDtypeStruct((TOK, FF), BF16), jax.ShapeDtypeStruct((FF, DH), F32)),
        in_specs=[vmem, vmem],
        out_specs=(anywhere, anywhere),
        scratch_shapes=[dma((PIECES + 1,))],
        compiler_params=pltpu.CompilerParams(vmem_limit_bytes=2**20),
    )(*results)


def solution(mesh):
    placed = (
        P(("dp", "col"), "row"),
        P(("dp", "row"), "col"),
        P(("dp", "row")),
        P(),
        P("row", "col"),
    )
    return jax.shard_map(
        body,
        mesh=mesh,
        in_specs=placed,
        out_specs=(P(("dp", "col"), "row"), P("row", ("col", "dp"))),
        check_vma=False,
    )
```

```python
import jax
import jax.numpy as jnp
from jax import lax
from jax.experimental import pallas as pl
from jax.experimental.pallas import tpu as pltpu
from jax.sharding import PartitionSpec as P

MESH = pl.DeviceIdType.MESH
BF16 = jnp.bfloat16
F32 = jnp.float32

TOK = 128
FF = 3584
D = 1024
DH = D // 2
A, S = 1536, 1024
AW, SW = 1280, 1152
FT = 512
TA, TS = 256, 384
NA, NS = AW // TA, SW // TS
NW = 4
WR = S // 2 // NW
MESSAGES = 96
PIECES = 7


def column(row_vector, n):
    on_diagonal = lax.broadcasted_iota(jnp.int32, (n, n), 0) == lax.broadcasted_iota(jnp.int32, (n, n), 1)
    return jnp.sum(jnp.where(on_diagonal, jnp.broadcast_to(row_vector, (n, n)), 0.0), axis=1, keepdims=True)


def kernel(
    h_ref, c_ref, lang_ref, counts_ref, w_ref,
    gh_ref, gw_ref,
    wa, ws, wx, ha, hs, call, pa, ps, ra2, rs2, ra1, rs1, rax, rsx, gsa, gra, gss, grs, xst, xrv, xsum, xin, lang, counts, cin,
    ss, rs, sem_a, sem_s, sem_x, ls,
):
    dp, row, col = lax.axis_index("dp"), lax.axis_index("row"), lax.axis_index("col")
    xl, y = row // 4, row % 4
    z, h = col // 2, col % 2
    q = 1 - h
    x = h * 2 + xl
    xp, xm, xo = (x + 1) % 4, (x + 3) % 4, (x + 2) % 4
    zp, zm, zo = (z + 1) % 4, (z + 3) % 4, (z + 2) % 4
    yp, ym, yo = (y + 1) % 4, (y + 3) % 4, (y + 2) % 4

    def device(at_x, at_y, at_z):
        return (dp, (at_x % 2) * 4 + at_y, at_z * 2 + at_x // 2)

    to_zp, to_zm = device(x, y, zp), device(x, y, zm)
    to_yp, to_ym = device(x, yp, z), device(x, ym, z)
    to_xp, to_xm, to_x2 = device(xp, y, z), device(xm, y, z), device(xo, y, z)
    to_dp = (1 - dp, row, col)
    neighbours = (to_zp, to_zm, to_yp, to_ym, to_xp, to_xm, to_x2, to_dp)

    barrier = pltpu.get_barrier_semaphore()
    for neighbour in neighbours:
        pl.semaphore_signal(barrier, inc=1, device_id=neighbour, device_id_type=MESH)

    s_own = pl.multiple_of(A + S * h, S // 2)
    s_other = pl.multiple_of(A + S * q, S // 2)
    sw_own = pl.multiple_of(AW + SW * h, 128)
    sw_other = pl.multiple_of(AW + SW * q, 128)
    h_a, h_s, h_o = (h_ref.at[:, pl.ds(at, n)] for at, n in ((0, AW), (sw_own, SW), (sw_other, SW)))
    small = [
        pltpu.make_async_copy(lang_ref, lang, ls.at[4]),
        pltpu.make_async_copy(counts_ref, counts, ls.at[5]),
        pltpu.make_async_copy(c_ref, cin, ls.at[6]),
    ]
    loads = [
        pltpu.make_async_copy(h_a, ha.at[col], ls.at[0]),
        pltpu.make_async_copy(h_s, hs.at[col], ls.at[1]),
        pltpu.make_async_copy(w_ref.at[pl.ds(0, A), :], wa, ls.at[2]),
        pltpu.make_async_copy(w_ref.at[pl.ds(s_own, S), :], ws, ls.at[3]),
    ]
    for load in small + loads:
        load.start()
    for load in small:
        load.wait()

    lang_weight = column(jnp.sqrt(512.0 / counts[...].astype(F32)), 32)
    matches = lang[...] == lax.broadcasted_iota(jnp.int32, (32, TOK), 0)
    weight_row = jnp.sum(jnp.where(matches, lang_weight, 0.0), axis=0, keepdims=True)
    token_weight = column(weight_row, TOK)
    call[h, row] = (cin[...].astype(F32) * token_weight).astype(BF16)

    pl.semaphore_wait(barrier, len(neighbours))

    sent = []

    def send(src, dst, to):
        i = len(sent)
        copy = pltpu.make_async_remote_copy(
            src_ref=src, dst_ref=dst, send_sem=ss.at[i], recv_sem=rs.at[i], device_id=to, device_id_type=MESH
        )
        copy.start()
        sent.append(copy)
        return copy

    def got(*copies):
        for copy in copies:
            copy.wait_recv()

    def cots_whole(at_x, at_y, to):
        at = call.at[at_x // 2, (at_x % 2) * 4 + at_y]
        return send(at, at, to)

    def cots_half(at_x, at_y, half, to):
        at = call.at[at_x // 2, (at_x % 2) * 4 + at_y, pl.ds(half * (TOK // 2), TOK // 2), :]
        return send(at, at, to)

    def cots_along_y(at_x):
        return [cots_whole(at_x, y, to_yp), cots_whole(at_x, y, to_ym)]

    def cots_far_y(at_x):
        return [cots_half(at_x, ym, 0, to_yp), cots_half(at_x, yp, 1, to_ym)]

    def hidden_on(ref, hh, n, cut):
        at_m, at_p = ref.at[zm * 2 + hh, :, pl.ds(0, cut)], ref.at[zp * 2 + hh, :, pl.ds(cut, n - cut)]
        return [send(at_m, at_m, to_zp), send(at_p, at_p, to_zm)]

    def hidden_halves(ref, at, n):
        lo, hi = ref.at[at, :, pl.ds(0, n // 2)], ref.at[at, :, pl.ds(n // 2, n // 2)]
        return [send(lo, lo, to_zp), send(hi, hi, to_zm)], [send(hi, hi, to_zp), send(lo, lo, to_zm)]

    def hidden_round(src, ref, at):
        return [send(src, ref.at[at], to_zp), send(src, ref.at[at], to_zm)]

    par = z * 2 + q
    c_x = [cots_whole(x, y, to_xp), cots_whole(x, y, to_xm)]
    own_s = hidden_round(h_s, hs, col)
    c_y = cots_along_y(x)
    x_s = send(h_o, hs.at[col], to_x2)
    own_a = hidden_round(h_a, ha, col)

    got(*c_x)
    c_x2 = [cots_half(xm, y, 0, to_xp), cots_half(xp, y, 1, to_xm)]
    c_ym, c_yp = cots_along_y(xm), cots_along_y(xp)
    x_a = send(h_a, ha.at[col], to_x2)
    w_x = []
    for i in range(NW):
        rows = pl.multiple_of(dp * (S // 2) + i * WR, WR)
        w_x.append(send(w_ref.at[pl.ds(pl.multiple_of(s_other + rows, WR), WR), :], wx.at[pl.ds(rows, WR), :], to_x2))
    got(*own_s)
    far_own_s = hidden_on(hs, h, SW, 640)
    got(*c_y)
    c_y2 = cots_far_y(x)
    got(x_s)
    par_s = hidden_round(hs.at[par], hs, par)
    got(*c_x2)
    c_yo = cots_along_y(xo)
    got(*own_a)
    far_own_a = hidden_on(ha, h, AW, AW // 2)
    got(*c_ym)
    c_ym2 = cots_far_y(xm)
    got(*c_yp)
    c_yp2 = cots_far_y(xp)
    got(*par_s)
    far_par_s = hidden_on(hs, q, SW, 512)
    got(x_a)
    par_a, par_a2 = hidden_halves(ha, par, AW)
    got(*c_yo)
    c_yo2 = cots_far_y(xo)
    for load in loads:
        load.wait()
    got(*par_a)
    far_par_a = hidden_on(ha, q, AW, AW // 2)
    got(*c_y2, *c_ym2, *c_yp2, *c_yo2)

    def times_weight(cots, weight):
        return lax.dot_general(cots, weight, (((1,), (1,)), ((), ())), preferred_element_type=F32)

    def cots_of(hh, zd):
        return call[hh, pl.ds(zd * 2, 2)].reshape(2 * TOK, D)

    def terms_a(at, zd):
        def step(j, carry):
            units = pl.ds(pl.multiple_of(j * FT, FT), FT)
            pa[at, :, :, units] = times_weight(cots_of(h, zd), wa[units, :]).astype(BF16).reshape(2, TOK, FT)
            return carry
        lax.fori_loop(0, A // FT, step, 0)

    def terms_s(at, zd):
        def step(j, carry):
            units = pl.ds(pl.multiple_of(j * FT, FT), FT)
            both = times_weight(cots_of(h, zd), ws[units, :]) + times_weight(cots_of(q, zd), wx[units, :])
            ps[at, :, :, units] = both.astype(BF16).reshape(2, TOK, FT)
            return carry
        lax.fori_loop(0, S // FT, step, 0)

    def add(ref, at, *others):
        total = ref[at].astype(F32)
        for other, other_at in others:
            total = total + other[other_at].astype(F32)
        ref[at] = total.astype(BF16)

    everything = slice(None)

    def far(p, r2, hh, n):
        half = n // 2
        return [
            send(p.at[0, hh, :, pl.ds(0, half)], r2.at[hh, 0], to_zp),
            send(p.at[0, hh, :, pl.ds(half, half)], r2.at[hh, 1], to_zm),
        ]

    def near(p, r2, r1, hh, n):
        half = n // 2
        add(p, (1, hh, everything, slice(0, half)), (r2, (hh, 0)))
        add(p, (2, hh, everything, slice(half, n)), (r2, (hh, 1)))
        return [send(p.at[1, hh], r1.at[hh, 0], to_zp), send(p.at[2, hh], r1.at[hh, 1], to_zm)]

    def home(p, r1, hh):
        add(p, (3, hh), (r1, (hh, 0)), (r1, (hh, 1)))

    def product(ref, units, hh, part):
        hidden = ref[:, :, units].reshape(8 * TOK, units.size)
        cots = call[hh, :, :, pl.ds(pl.multiple_of(part * DH, DH), DH)].reshape(8 * TOK, DH)
        out = lax.dot_general(hidden, cots, (((0,), (0,)), ((), ())), preferred_element_type=F32)
        return out.astype(BF16)

    def to_other_core(st, rv, sems, j):
        return pltpu.make_async_remote_copy(
            src_ref=st.at[j], dst_ref=rv.at[j], send_sem=sems.at[0, j], recv_sem=sems.at[1, j],
            device_id=to_dp, device_id_type=MESH,
        )

    def partner_tile(j):
        units = pl.ds(j * TS, TS)
        xst[j] = product(hs, units, q, 1 - dp)
        to_other_core(xst, xrv, sem_x, j).start()
        xsum[j] = product(hs, units, q, dp)

    def own_tiles(ref, st, rv, sems, size, first, lo, hi):
        def step(j, carry):
            units = pl.ds(pl.multiple_of(j * size, 128), size)
            st[j] = product(ref, units, h, 1 - dp)
            to_other_core(st, rv, sems, j).start()
            gw_ref[pl.ds(pl.multiple_of(first + j * size, 128), size), :] = product(ref, units, h, dp).astype(F32)
            return carry
        lax.fori_loop(lo, hi, step, 0)

    def own_sums(st, rv, sems, size, first, n):
        def step(j, carry):
            to_other_core(st, rv, sems, j).wait()
            gw_ref[pl.ds(pl.multiple_of(first + j * size, 128), size), :] += rv[j].astype(F32)
            return carry
        lax.fori_loop(0, n, step, 0)

    terms_a(0, zo)
    far_aq = far(pa, ra2, q, A)
    far_ah = far(pa, ra2, h, A)
    got(*far_own_s, *far_par_s)
    returns = []

    def give_back(j):
        to_other_core(xst, xrv, sem_x, j).wait()
        add(xsum, j, (xrv, j))
        returns.append(send(xsum.at[j], xin.at[j], to_x2))

    for j in range(NS):
        partner_tile(j)
        if j:
            give_back(j - 1)
    give_back(NS - 1)
    terms_a(1, zp)
    terms_a(2, zm)
    w_dp = []
    for i in range(NW):
        got(w_x[i])
        rows = pl.ds(pl.multiple_of(dp * (S // 2) + i * WR, WR), WR)
        w_dp.append(send(wx.at[rows, :], wx.at[rows, :], to_dp))
    got(*far_aq)
    near_aq = near(pa, ra2, ra1, q, A)
    terms_a(3, z)
    got(*w_dp)
    terms_s(0, zo)
    far_sq = far(ps, rs2, q, S)
    far_sh = far(ps, rs2, h, S)
    terms_s(1, zp)
    terms_s(2, zm)
    got(*near_aq)
    home(pa, ra1, q)
    last_a = send(pa.at[3, q], rax, to_x2)
    got(*far_sq)
    near_sq = near(ps, rs2, rs1, q, S)
    got(*far_ah)
    near_ah = near(pa, ra2, ra1, h, A)
    got(*far_sh)
    near_sh = near(ps, rs2, rs1, h, S)
    terms_s(3, z)
    got(*far_own_a, *par_a2, *far_par_a)
    own_tiles(hs, gss, grs, sem_s, TS, sw_own, 0, NS)
    own_tiles(ha, gsa, gra, sem_a, TA, 0, 0, 1)
    got(*near_sq)
    home(ps, rs1, q)
    last_s = send(ps.at[3, q], gh_ref.at[:, pl.ds(s_own, S)], to_x2)
    own_tiles(ha, gsa, gra, sem_a, TA, 0, 1, NA)
    own_sums(gsa, gra, sem_a, TA, 0, NA)
    own_sums(gss, grs, sem_s, TS, sw_own, NS)
    got(*near_ah)
    home(pa, ra1, h)
    for j in range(NS):
        got(returns[j])
        gw_ref[pl.ds(pl.multiple_of(sw_other + j * TS, 128), TS), :] = xin[j].astype(F32)
    late = [*near_ah, *near_sh, last_a, last_s]
    for copy in sent:
        if all(copy is not other for other in late):
            copy.wait_send()
    got(last_a)
    add(pa, (3, h), (rax, everything))
    gh_ref[:, 0:A] = pa[3, h]
    got(*near_sh)
    home(ps, rs1, h)
    gh_ref[:, pl.ds(s_own, S)] = ps[3, h]
    got(last_s)

    for copy in late:
        copy.wait_send()


def write_out(gh_ref, gw_ref, gh_out, gw_out, sems):
    rows = FF // PIECES
    copies = [pltpu.make_async_copy(gh_ref, gh_out, sems.at[PIECES])]
    for i in range(PIECES):
        at = pl.ds(i * rows, rows)
        copies.append(pltpu.make_async_copy(gw_ref.at[at, :], gw_out.at[at, :], sems.at[i]))
    for copy in copies:
        copy.start()
    for copy in copies:
        copy.wait()


def body(hidden, cotangent, language, counts, weight):
    anywhere = pl.BlockSpec(memory_space=pl.ANY)
    vmem = pl.BlockSpec(memory_space=pltpu.VMEM)
    dma = pltpu.SemaphoreType.DMA
    results = pl.pallas_call(
        kernel,
        out_shape=(pltpu.VMEM((TOK, FF), BF16), pltpu.VMEM((FF, DH), F32)),
        in_specs=[anywhere] * 5,
        out_specs=(vmem, vmem),
        scratch_shapes=[
            pltpu.VMEM((A, D), BF16),
            pltpu.VMEM((S, D), BF16),
            pltpu.VMEM((S, D), BF16),
            pltpu.VMEM((8, TOK, AW), BF16),
            pltpu.VMEM((8, TOK, SW), BF16),
            pltpu.VMEM((2, 8, TOK, D), BF16),
            pltpu.VMEM((4, 2, TOK, A), BF16),
            pltpu.VMEM((4, 2, TOK, S), BF16),
            pltpu.VMEM((2, 2, TOK, A // 2), BF16),
            pltpu.VMEM((2, 2, TOK, S // 2), BF16),
            pltpu.VMEM((2, 2, TOK, A), BF16),
            pltpu.VMEM((2, 2, TOK, S), BF16),
            pltpu.VMEM((TOK, A), BF16),
            pltpu.VMEM((TOK, S), BF16),
            pltpu.VMEM((NA, TA, DH), BF16),
            pltpu.VMEM((NA, TA, DH), BF16),
            pltpu.VMEM((NS, TS, DH), BF16),
            pltpu.VMEM((NS, TS, DH), BF16),
            pltpu.VMEM((NS, TS, DH), BF16),
            pltpu.VMEM((NS, TS, DH), BF16),
            pltpu.VMEM((NS, TS, DH), BF16),
            pltpu.VMEM((NS, TS, DH), BF16),
            pltpu.VMEM((1, TOK), jnp.int32),
            pltpu.VMEM((1, 32), jnp.int32),
            pltpu.VMEM((TOK, D), BF16),
            dma((MESSAGES,)),
            dma((MESSAGES,)),
            dma((2, NA)),
            dma((2, NS)),
            dma((2, NS)),
            dma((7,)),
        ],
        compiler_params=pltpu.CompilerParams(
            collective_id=0, has_side_effects=True, vmem_limit_bytes=54 * 2**20
        ),
        cost_estimate=pl.CostEstimate(flops=4 * 1024 * FF * D, bytes_accessed=24 * 2**20, transcendentals=32),
    )(hidden, cotangent, language.reshape(1, TOK), counts.reshape(1, 32), weight)
    return pl.pallas_call(
        write_out,
        out_shape=(jax.ShapeDtypeStruct((TOK, FF), BF16), jax.ShapeDtypeStruct((FF, DH), F32)),
        in_specs=[vmem, vmem],
        out_specs=(anywhere, anywhere),
        scratch_shapes=[dma((PIECES + 1,))],
        compiler_params=pltpu.CompilerParams(vmem_limit_bytes=2**20),
    )(*results)


def solution(mesh):
    placed = (
        P(("dp", "col"), "row"),
        P(("dp", "row"), "col"),
        P(("dp", "row")),
        P(),
        P("row", "col"),
    )
    return jax.shard_map(
        body,
        mesh=mesh,
        in_specs=placed,
        out_specs=(P(("dp", "col"), "row"), P("row", ("col", "dp"))),
        check_vma=False,
    )
```
